32 devices in a mesh: section: 2 (over core), dp: 16 (over z, y, x).
Axes of the slice: x: 2, y: 2, z: 4, core: 2. Of those that a mesh axis runs over, the one named last changes fastest.
Arguments:
- reduce_weight: bfloat16 [2048, 512], P('dp'), may hold values from -0.125 to 0.125
- dilated_weight: bfloat16 [4608, 512], P('dp'), may hold values from -0.09375 to 0.09375
- expand_weight: bfloat16 [512, 2048], P('dp'), may hold values from -0.25 to 0.25
- reduce_gain: float32 [512], replicated, may hold values from 0.5 to 1.5
- reduce_bias: float32 [512], replicated, may hold values from -1.5 to 1.5
- dilated_gain: float32 [512], replicated, may hold values from 0.5 to 1.5
- dilated_bias: float32 [512], replicated, may hold values from -1.5 to 1.5
- expand_gain: float32 [2048], replicated, may hold values from 0.5 to 1.5
- expand_bias: float32 [2048], replicated, may hold values from -1.5 to 1.5
- head_conv: bfloat16 [18432, 768], P('dp'), may hold values from -0.046875 to 0.046875
- head_gain: float32 [768], replicated, may hold values from 0.5 to 1.5
- head_bias: float32 [768], replicated, may hold values from -1.5 to 1.5
- seg_proj: bfloat16 [256, 13], replicated, may hold values from -0.75 to 0.75
- depth_proj: bfloat16 [256, 1], replicated, may hold values from -1.5 to 1.5
- normal_proj: bfloat16 [256, 3], replicated, may hold values from -0.75 to 0.75
- small_feats: bfloat16 [1536, 2048], P('dp'), may hold values from -6 to 6
- small_labels: int32 [1536], P('dp'), may hold values from -1 to 12
- small_depth: float32 [1536], P('dp'), may hold values from 0.5 to 10
- small_normals: float32 [3, 1536], P(None, 'dp'), may hold values from -3 to 3
- small_depth_valid: int32 [1536], P('dp'), may hold values 0 or 1
- small_normal_valid: int32 [1536], P('dp'), may hold values 0 or 1
- large_feats: bfloat16 [2560, 2048], P('dp'), may hold values from -6 to 6
- large_labels: int32 [2560], P('dp'), may hold values from -1 to 12
- large_depth: float32 [2560], P('dp'), may hold values from 0.5 to 10
- large_normals: float32 [3, 2560], P(None, 'dp'), may hold values from -3 to 3
- large_depth_valid: int32 [2560], P('dp'), may hold values 0 or 1
- large_normal_valid: int32 [2560], P('dp'), may hold values 0 or 1
Outputs:
- small_out: bfloat16 [1536, 2048], P('dp')
- large_out: bfloat16 [2560, 2048], P('dp')
- small_input_grad: float32 [1536, 2048], P('dp', 'section')
- large_input_grad: float32 [2560, 2048], P('dp', 'section')
- reduce_weight_grad: float32 [2048, 512], P('dp')
- dilated_weight_grad: float32 [4608, 512], P('dp')
- expand_weight_grad: float32 [512, 2048], P('dp')
- reduce_gain_grad: float32 [512], replicated
- reduce_bias_grad: float32 [512], replicated
- dilated_gain_grad: float32 [512], replicated
- dilated_bias_grad: float32 [512], replicated
- expand_gain_grad: float32 [2048], replicated
- expand_bias_grad: float32 [2048], replicated
- head_conv_grad: float32 [18432, 768], P('dp')
- head_gain_grad: float32 [768], replicated
- head_bias_grad: float32 [768], replicated
- seg_proj_grad: float32 [256, 13], replicated
- depth_proj_grad: float32 [256, 1], replicated
- normal_proj_grad: float32 [256, 3], replicated
The draws below stay inside these ranges and needn't reach their ends.
All inputs are finite; a program needn't handle non-finite values. No bound on the sum of `small_depth_valid` or of `small_normal_valid` or of `large_depth_valid` or of `large_normal_valid` on one device may be relied on, other than what follows from the above.
Results may differ from the reference program's by a relative error of at most 0.02.
Values may be sent and summed in bfloat16 or wider, within the bound.
A program may use at most 320 MiB of HBM per device.

```python
import math
import jax
import jax.numpy as jnp
from jax import lax

C = 2048
BOT = 512
HEADW = 256
NCLS = 13
WS = 48
WL = 80
HS = 36
HL = 60
PIX_S = 1536
PIX_L = 2560


def place_ends(values, rng, smallest, largest):
    place = [jax.random.randint(jax.random.fold_in(rng, axis), (), 0, length) for axis, length in enumerate(values.shape)]
    longest = values.shape.index(max(values.shape))
    neighbour = place[:longest] + [(place[longest] + 1) % values.shape[longest]] + place[longest + 1:]
    return values.at[tuple(place)].set(smallest).at[tuple(neighbour)].set(largest)


def strengthened(values, key, source, target, parts, factor):
    def block_of(dim):
        return (jnp.arange(values.shape[dim]) // (values.shape[dim] // parts)).reshape((-1,) + (1,) * (values.ndim - 1 - dim))

    first = jax.random.permutation(key, parts)[block_of(target)]
    far = (block_of(target) + parts // 2) % parts
    return jnp.where((block_of(source) == first) | (block_of(source) == far), factor * values, values)


def shard_levels(own_key, shape, shards, smallest, largest):
    factor_of = 1.0
    for dim, blocks in shards:
        heights = jax.random.uniform(jax.random.fold_in(jax.random.fold_in(own_key, 6), dim), (blocks,), jnp.float32, smallest / len(shards), largest / len(shards))
        factor_of = factor_of * jnp.repeat(jnp.exp(heights), shape[dim] // blocks).reshape((-1,) + (1,) * (len(shape) - 1 - dim))
    return factor_of


def centred(key, dims, scale, limit, pieces=(), held_as=jnp.bfloat16):
    drawn = scale * jax.random.normal(key, dims, jnp.float32)
    if pieces:
        drawn = drawn * shard_levels(key, dims, pieces, -0.22, 0.18)
    return jnp.clip(drawn, -limit, limit).astype(held_as)


def gaussian_with(key, extent, scale, most, shards, heavy, kind=jnp.bfloat16):
    drawn = scale * jax.random.normal(key, extent, jnp.float32)
    if shards:
        drawn = drawn * shard_levels(key, extent, shards, -0.22, 0.18)
    return jnp.clip(strengthened(drawn, jax.random.fold_in(key, 3), *heavy), -most, most).astype(kind)


def setup_inputs(seed: int = 0) -> dict:
    arg_keys = jax.random.split(jax.random.key(seed), 28)
    return {
        "reduce_weight": centred(arg_keys[0], (C, BOT), C ** -0.5, 0.125, ((0, 16),)),
        "dilated_weight": centred(arg_keys[1], (9 * BOT, BOT), (9 * BOT) ** -0.5, 0.09375, ((0, 16),)),
        "expand_weight": centred(arg_keys[2], (BOT, C), BOT ** -0.5, 0.25, ((0, 16),)),
        "reduce_gain": jnp.clip(1.0 + 0.1 * jax.random.normal(arg_keys[3], (BOT,), jnp.float32), 0.5, 1.5),
        "reduce_bias": centred(arg_keys[4], (BOT,), 0.3, 1.5, (), jnp.float32),
        "dilated_gain": jnp.clip(1.0 + 0.1 * jax.random.normal(arg_keys[5], (BOT,), jnp.float32), 0.5, 1.5),
        "dilated_bias": centred(arg_keys[6], (BOT,), 0.3, 1.5, (), jnp.float32),
        "expand_gain": jnp.clip(1.0 + 0.1 * jax.random.normal(arg_keys[7], (C,), jnp.float32), 0.5, 1.5),
        "expand_bias": centred(arg_keys[8], (C,), 0.3, 1.5, (), jnp.float32),
        "head_conv": centred(arg_keys[9], (9 * C, 3 * HEADW), (9 * C) ** -0.5, 0.046875, ((0, 16),)),
        "head_gain": jnp.clip(1.0 + 0.1 * jax.random.normal(arg_keys[10], (3 * HEADW,), jnp.float32), 0.5, 1.5),
        "head_bias": centred(arg_keys[11], (3 * HEADW,), 0.3, 1.5, (), jnp.float32),
        "seg_proj": centred(arg_keys[12], (HEADW, NCLS), (HEADW // 4) ** -0.5, 0.75),
        "depth_proj": centred(arg_keys[13], (HEADW, 1), (HEADW // 16) ** -0.5, 1.5),
        "normal_proj": centred(arg_keys[14], (HEADW, 3), (HEADW // 4) ** -0.5, 0.75),
        "small_feats": gaussian_with(arg_keys[15], (PIX_S, C), 1.0, 6.0, ((0, 16),), (0, 1, 16, 2.0)),
        "small_labels": place_ends(jax.random.randint(arg_keys[16], (PIX_S,), -1, NCLS), jax.random.fold_in(arg_keys[16], 1), -1, NCLS - 1).astype(jnp.int32),
        "small_depth": jnp.clip(jnp.exp(math.log(10.0) - 2.9957323 * jax.random.uniform(arg_keys[17], (PIX_S,), jnp.float32) ** shard_levels(arg_keys[17], (PIX_S,), ((0, 16),), -0.2, 0.2)), 0.5, 10.0),
        "small_normals": centred(arg_keys[18], (3, PIX_S), 0.6, 3.0, ((1, 16),), jnp.float32),
        "small_depth_valid": place_ends((jax.random.randint(arg_keys[19], (PIX_S,), 0, 5) < 4).astype(jnp.int32), jax.random.fold_in(arg_keys[19], 1), 0, 1),
        "small_normal_valid": place_ends((jax.random.randint(arg_keys[20], (PIX_S,), 0, 5) < 4).astype(jnp.int32), jax.random.fold_in(arg_keys[20], 1), 0, 1),
        "large_feats": gaussian_with(arg_keys[21], (PIX_L, C), 1.0, 6.0, ((0, 16),), (0, 1, 16, 2.0)),
        "large_labels": place_ends(jax.random.randint(arg_keys[22], (PIX_L,), -1, NCLS), jax.random.fold_in(arg_keys[22], 1), -1, NCLS - 1).astype(jnp.int32),
        "large_depth": jnp.clip(jnp.exp(math.log(10.0) - 2.9957323 * jax.random.uniform(arg_keys[23], (PIX_L,), jnp.float32) ** shard_levels(arg_keys[23], (PIX_L,), ((0, 16),), -0.2, 0.2)), 0.5, 10.0),
        "large_normals": centred(arg_keys[24], (3, PIX_L), 0.6, 3.0, ((1, 16),), jnp.float32),
        "large_depth_valid": place_ends((jax.random.randint(arg_keys[25], (PIX_L,), 0, 5) < 4).astype(jnp.int32), jax.random.fold_in(arg_keys[25], 1), 0, 1),
        "large_normal_valid": place_ends((jax.random.randint(arg_keys[26], (PIX_L,), 0, 5) < 4).astype(jnp.int32), jax.random.fold_in(arg_keys[26], 1), 0, 1),
    }


EPS = 1e-05
RIDGE = 0.1
SWEEPS = 5
HIGH = lax.Precision.HIGHEST

@jax.custom_vjp
def low(v):
    return lax.optimization_barrier(v.astype(jnp.bfloat16)).astype(jnp.float32)

@jax.custom_vjp
def low_back(v):
    return v

def low_keep(v):
    return (low(v), None)

def low_pass(kept, grad):
    return (grad,)

def back_keep(v):
    return (v, None)

def back_low(kept, grad):
    return (low(grad),)
low.defvjp(low_keep, low_pass)
low_back.defvjp(back_keep, back_low)

def matmul_high(left, right):
    return jnp.dot(left, right, precision=HIGH, preferred_element_type=jnp.float32)

def small_product(left, right):
    return lax.optimization_barrier(jnp.sum(left[:, :, None] * right[None, :, :], axis=1))

def row_masks(row_count, strip, height, start):
    local = start + jnp.arange(row_count, dtype=jnp.int32)
    stacked = []
    for tap_row in range(3):
        other = local + 2 * (tap_row - 1)
        keep = (other >= 0) & (other < strip) & (other // height == local // height)
        stacked.append(keep.astype(jnp.float32))
    return jnp.stack(stacked)

def align_weights(gram):
    identity = jnp.eye(3, dtype=jnp.float32)
    matrix = gram + RIDGE * jnp.trace(gram) / 3.0 * identity
    vectors = identity
    for sweep in range(SWEEPS):
        for first_i, second_i in ((0, 1), (0, 2), (1, 2)):
            angle = 0.5 * jnp.arctan2(2.0 * matrix[first_i, second_i], matrix[second_i, second_i] - matrix[first_i, first_i])
            cosine = jnp.cos(angle)
            sine = jnp.sin(angle)
            rotate = identity.at[first_i, first_i].set(cosine).at[second_i, second_i].set(cosine)
            rotate = rotate.at[first_i, second_i].set(sine).at[second_i, first_i].set(-sine)
            matrix = small_product(rotate.T, small_product(matrix, rotate))
            vectors = small_product(vectors, rotate)
    values = jnp.diagonal(matrix)
    inverse_root = small_product(vectors * lax.rsqrt(values)[None, :], vectors.T)
    return jnp.sqrt(jnp.min(values)) * lax.optimization_barrier(jnp.sum(inverse_root, axis=1))

def dilated_conv(grid, kernel, height):
    strip, width, channels = grid.shape
    masks = row_masks(strip, strip, height, 0)
    padded = jnp.pad(grid, ((2, 2), (2, 2), (0, 0)))
    span = strip // 8
    outputs = kernel.shape[1]

    def one_block(index):
        first_row = index * span
        window = lax.dynamic_slice_in_dim(padded, first_row, span + 4, 0)
        local_masks = lax.dynamic_slice_in_dim(masks, first_row, span, 1)
        result = jnp.zeros((span * width, outputs), jnp.float32)
        for tap_row in range(3):
            for tap_col in range(3):
                piece = window[2 * tap_row:2 * tap_row + span, 2 * tap_col:2 * tap_col + width, :]
                piece = piece * local_masks[tap_row][:, None, None]
                tap = 3 * tap_row + tap_col
                result = result + matmul_high(piece.reshape(span * width, channels), kernel[tap * channels:(tap + 1) * channels])
        return result
    blocks = lax.map(jax.checkpoint(one_block), jnp.arange(8, dtype=jnp.int32))
    return blocks.reshape(strip * width, outputs)

def batch_norm(pre, gain, bias):
    mean = lax.optimization_barrier(jnp.mean(pre, axis=0))
    spread = lax.optimization_barrier(jnp.mean(pre * pre, axis=0)) - mean * mean
    return (pre - mean) * lax.rsqrt(spread + EPS) * gain + bias

def trunk(params, inputs, width, height):
    reduce_w, dilated_w, expand_w, reduce_gain, reduce_bias, dilated_gain, dilated_bias, expand_gain, expand_bias = params
    strip = inputs.shape[0] // width
    pre_one = low_back(matmul_high(inputs, reduce_w))
    act_one = low(jax.nn.silu(batch_norm(pre_one, reduce_gain, reduce_bias)))
    pre_two = low_back(dilated_conv(act_one.reshape(strip, width, BOT), dilated_w, height))
    act_two = low(jax.nn.silu(batch_norm(pre_two, dilated_gain, dilated_bias)))
    pre_three = low_back(matmul_high(act_two, expand_w))
    return jax.nn.silu(batch_norm(pre_three, expand_gain, expand_bias) + inputs)

def heads(params, features, labels, depth, normals, depth_valid, normal_valid, width, height):
    conv_w, gain, bias, seg_w, depth_w, normal_w = params
    strip = features.shape[0] // width
    pre = low_back(dilated_conv(features.reshape(strip, width, C), conv_w, height))
    act = low(jax.nn.silu(batch_norm(pre, gain, bias)))
    logits = matmul_high(act[:, :HEADW], seg_w)
    depth_pred = matmul_high(act[:, HEADW:2 * HEADW], depth_w)[:, 0]
    normal_pred = matmul_high(act[:, 2 * HEADW:], normal_w)
    seg_valid = (labels >= 0).astype(jnp.float32)
    seg_count = jnp.maximum(jnp.sum(seg_valid), 1.0)
    picked = lax.optimization_barrier(jnp.sum(jnp.where(labels[:, None] == jnp.arange(NCLS, dtype=jnp.int32)[None, :], logits, 0.0), axis=1))
    loss_seg = jnp.sum(seg_valid * (jax.nn.logsumexp(logits, axis=1) - picked)) / seg_count
    depth_keep = depth_valid.astype(jnp.float32)
    depth_count = jnp.maximum(jnp.sum(depth_keep), 1.0)
    gap = depth_pred - depth
    loss_depth = jnp.sum(depth_keep * (jnp.sqrt(gap * gap + 1.0) - 1.0)) / depth_count
    normal_keep = normal_valid.astype(jnp.float32)
    normal_count = jnp.maximum(jnp.sum(normal_keep), 1.0)
    radius = jnp.sqrt(lax.optimization_barrier(jnp.sum(normal_pred * normal_pred, axis=1)) + 1.0)
    cosine = lax.optimization_barrier(jnp.sum(normal_pred * normals.T, axis=1)) / radius
    loss_normal = jnp.sum(normal_keep * (1.0 - cosine)) / normal_count
    return (loss_seg, loss_depth, loss_normal)

def add_trees(first, second):
    return jax.tree.map(lambda left, right: left + right, first, second)

def group_pass(trunk_params, head_params, feats, labels, depth, normals, depth_valid, normal_valid, width, height):
    inputs = feats.astype(jnp.float32)

    def trunk_fn(params, values):
        return trunk(params, values, width, height)
    output, trunk_back = jax.vjp(trunk_fn, trunk_params, inputs)
    sent = lax.optimization_barrier(output.astype(jnp.bfloat16)).astype(jnp.float32)

    def head_fn(params, values):
        return heads(params, values, labels, depth, normals, depth_valid, normal_valid, width, height)
    losses, head_back = jax.vjp(head_fn, head_params, sent)
    task_grads = []
    head_total = None
    for task in range(3):
        cotangent = tuple((jnp.asarray(1.0 if other == task else 0.0, jnp.float32) for other in range(3)))
        param_grads, feature_grad = head_back(cotangent)
        task_grads.append(feature_grad)
        head_total = param_grads if head_total is None else add_trees(head_total, param_grads)
    gram = jnp.stack([jnp.stack([jnp.sum(task_grads[row] * task_grads[col]) for col in range(3)]) for row in range(3)])
    alpha = align_weights(gram)
    combined = alpha[0] * task_grads[0] + alpha[1] * task_grads[1] + alpha[2] * task_grads[2]
    sent_back = lax.optimization_barrier(combined.astype(jnp.bfloat16)).astype(jnp.float32)
    trunk_grads, input_grad = trunk_back(sent_back)
    return (output.astype(jnp.bfloat16), input_grad, trunk_grads, head_total)

def reference(reduce_weight, dilated_weight, expand_weight, reduce_gain, reduce_bias, dilated_gain, dilated_bias, expand_gain, expand_bias, head_conv, head_gain, head_bias, seg_proj, depth_proj, normal_proj, small_feats, small_labels, small_depth, small_normals, small_depth_valid, small_normal_valid, large_feats, large_labels, large_depth, large_normals, large_depth_valid, large_normal_valid):
    trunk_params = tuple((value.astype(jnp.float32) for value in (reduce_weight, dilated_weight, expand_weight, reduce_gain, reduce_bias, dilated_gain, dilated_bias, expand_gain, expand_bias)))
    head_params = tuple((value.astype(jnp.float32) for value in (head_conv, head_gain, head_bias, seg_proj, depth_proj, normal_proj)))
    small_out, small_grad, small_trunk, small_head = group_pass(trunk_params, head_params, small_feats, small_labels, small_depth, small_normals, small_depth_valid, small_normal_valid, WS, HS)
    large_out, large_grad, large_trunk, large_head = group_pass(trunk_params, head_params, large_feats, large_labels, large_depth, large_normals, large_depth_valid, large_normal_valid, WL, HL)
    trunk_total = add_trees(small_trunk, large_trunk)
    head_total = add_trees(small_head, large_head)
    return (small_out, large_out, small_grad, large_grad, trunk_total[0], trunk_total[1], trunk_total[2], trunk_total[3], trunk_total[4], trunk_total[5], trunk_total[6], trunk_total[7], trunk_total[8], head_total[0], head_total[1], head_total[2], head_total[3], head_total[4], head_total[5])
```

```python
import functools

import jax
import jax.numpy as jnp
from jax import lax
from jax.experimental import pallas as pl
from jax.experimental.pallas import tpu as pltpu
from jax.sharding import PartitionSpec as P

C = 2048
BOT = 512
HEADW = 256
NCLS = 13
WS = 48
WL = 80
HS = 36
HL = 60

EPS = 1e-05
RIDGE = 0.1
SWEEPS = 5

F32 = jnp.float32
BF16 = jnp.bfloat16
MESH = pl.DeviceIdType.MESH

LINE = WS + WL
SEGMENTS = ((0, WS), (WS, WL))
HEIGHTS = (HS, HL)
PIX = 2 * LINE
TEAM = 8
CH = C // TEAM
HALF = BOT // 2
WIDE = C // 2
HEADS = 3 * HEADW
TAPS = 9
PROJ = 32
DEPTH_ROW = 16
NORMAL_ROW = 24

NN = (((1,), (0,)), ((), ()))
NT = (((1,), (1,)), ((), ()))
TN = (((0,), (0,)), ((), ()))


def mm(left, right, dims=NN):
    return lax.dot_general(left, right, dims, preferred_element_type=F32)


def flip(rank, bits):
    out = rank
    for bit in (1, 2, 4):
        if bits & bit:
            out = out + bit * (1 - 2 * ((rank // bit) % 2))
    return out


def sigmoid(value):
    return 1.0 / (1.0 + jnp.exp(-value))


def silu(value):
    return value * sigmoid(value)


def slope(value):
    sigma = sigmoid(value)
    return sigma * (1.0 + value * (1.0 - sigma))


def seg_rows(lines):
    for line in range(lines):
        for group, (start, length) in enumerate(SEGMENTS):
            yield group, slice(line * LINE + start, line * LINE + start + length)


def position(rows):
    return lax.broadcasted_iota(jnp.int32, (rows, 1), 0) % LINE


def column_mask(rows, tap_col):
    place = position(rows)
    small = place < WS
    column = jnp.where(small, place, place - WS) + (2 * tap_col - 2)
    width = jnp.where(small, WS, WL)
    return ((column >= 0) & (column < width)).astype(F32)


def sideways(value, tap_col):
    rows = value.shape[0]
    if tap_col == 1:
        return value
    return pltpu.roll(value, (2 - 2 * tap_col) % rows, 0) * column_mask(rows, tap_col)


def jacobi_weights(gram):
    third = (gram[0, 0] + gram[1, 1] + gram[2, 2]) / 3.0 * RIDGE
    matrix = {(i, j): gram[min(i, j), max(i, j)] + (third if i == j else 0.0) for i in range(3) for j in range(3)}
    one, zero = jnp.ones_like(third), jnp.zeros_like(third)
    vectors = {(i, j): one if i == j else zero for i in range(3) for j in range(3)}
    for _ in range(SWEEPS):
        for p, q in ((0, 1), (0, 2), (1, 2)):
            up = 2.0 * matrix[p, q]
            across = matrix[q, q] - matrix[p, p]
            scale = jnp.maximum(jnp.abs(up), jnp.abs(across))
            still = scale == 0.0
            scale = jnp.where(still, 1.0, scale)
            up, across = up / scale, across / scale
            length = jnp.where(still, 1.0, jnp.sqrt(up * up + across * across))
            larger = jnp.sqrt(0.5 + 0.5 * jnp.abs(across) / length)
            smaller = 0.5 * up / (length * larger)
            sign = jnp.where(up < 0.0, -1.0, 1.0)
            cosine = jnp.where(still, 1.0, jnp.where(across >= 0.0, larger, jnp.abs(smaller)))
            sine = jnp.where(still, 0.0, jnp.where(across >= 0.0, smaller, sign * larger))
            for i in range(3):
                first, second = matrix[i, p], matrix[i, q]
                matrix[i, p] = first * cosine - second * sine
                matrix[i, q] = first * sine + second * cosine
                first, second = vectors[i, p], vectors[i, q]
                vectors[i, p] = first * cosine - second * sine
                vectors[i, q] = first * sine + second * cosine
            for j in range(3):
                first, second = matrix[p, j], matrix[q, j]
                matrix[p, j] = first * cosine - second * sine
                matrix[q, j] = first * sine + second * cosine
    values = [matrix[i, i] for i in range(3)]
    least = jnp.sqrt(jnp.minimum(jnp.minimum(values[0], values[1]), values[2]))
    alphas = []
    roots = [lax.rsqrt(value) for value in values]
    sums = [vectors[0, k] + vectors[1, k] + vectors[2, k] for k in range(3)]
    for t in range(3):
        alphas.append(least * sum(vectors[t, k] * roots[k] * sums[k] for k in range(3)))
    return alphas


class Links:
    def __init__(self, send, recv, partner):
        self.send, self.recv, self.partner = send, recv, partner
        self.used_send = self.used_recv = 0
        self.open = []

    def slots(self, count=1):
        first = self.used_recv
        self.used_recv += count
        assert self.used_recv <= self.recv.shape[0]
        return first

    def outs(self, count=1):
        first = self.used_send
        self.used_send += count
        assert self.used_send <= self.send.shape[0]
        return first

    def copy(self, src, dst, device, out, slot):
        return pltpu.make_async_remote_copy(
            src_ref=src, dst_ref=dst, send_sem=self.send.at[out], recv_sem=self.recv.at[slot],
            device_id=device, device_id_type=MESH,
        )

    def put(self, src, dst, device, slot, when=None):
        out = self.outs()
        if when is not None:
            device = tuple(jnp.where(when, to, near) for to, near in zip(device, self.partner))
        make = functools.partial(self.copy, src, dst, device, out, slot)
        if when is None:
            make().start()
            done = lambda: make().wait_send()
        else:
            pl.when(when)(lambda: make().start())
            done = lambda: pl.when(when)(lambda: make().wait_send())
        self.open.append(done)
        return done

    def put_or_keep(self, src, dst, device, slot, mine, when=True):
        pl.when(when & mine)(lambda: pltpu.make_async_copy(src, dst, self.recv.at[slot]).start())
        return self.put(src, dst, device, slot, when & jnp.logical_not(mine))

    def landed(self, dst, slot, when=None):
        wait = lambda: pltpu.make_async_copy(dst, dst, self.recv.at[slot]).wait()
        if when is None:
            wait()
        else:
            pl.when(when)(wait)

    def close(self):
        for done in self.open:
            done()
        self.open = []


def pieces(ref, start, count):
    rows = ref.shape[2]
    at = start
    while at < start + count:
        shard, first = at // rows, at % rows
        length = min(rows - first, start + count - at)
        yield (shard // 4, shard % 4, slice(first, first + length)), slice(at - start, at - start + length)
        at += length


def take_rows(ref, start, count):
    if len(ref.shape) == 2:
        return ref[start:start + count, :]
    found = [ref[(*place, slice(None))] for place, _ in pieces(ref, start, count)]
    return found[0] if len(found) == 1 else jnp.concatenate(found, axis=0)


def put_rows(ref, start, value):
    if len(ref.shape) == 2:
        ref[start:start + value.shape[0], :] = value
        return
    for place, rows in pieces(ref, start, value.shape[0]):
        ref[(*place, slice(None))] = value[rows, :]


def several(count, body):
    if count <= 4:
        for index in range(count):
            body(index)
    else:
        lax.fori_loop(0, count, lambda index, carry: (body(index), carry)[1], 0)


class Shapes:
    def __init__(self, dp):
        self.dp = dp
        self.planes = dp // 4
        self.teams = dp // TEAM
        self.unit = C // dp
        self.units_half = dp // (2 * TEAM)
        self.rows = (C // dp, TAPS * BOT // dp, BOT // dp)
        self.wide = (HALF, HALF, WIDE)
        self.full = (C, TAPS * BOT, BOT)
        self.inside = all(rows % 32 == 0 for rows in self.rows)
        self.borders = 2 * dp > min(HEIGHTS)


def scratch_of(shape):
    planes = shape.planes
    table = {
        "x": ((PIX, C), BF16),
        "xh": ((PIX, WIDE), BF16),
        "wback": ((planes // 2, 4, C // shape.dp, HALF) if shape.inside else (WIDE, HALF), BF16),
        "kernel": ((TAPS, 2, CH // 2, HEADS), BF16),
        "pre1": ((PIX, HALF), F32),
        "pre2": ((PIX, HALF), F32),
        "pre3": ((PIX, WIDE), F32),
        "act1": ((3, 2, PIX, HALF), BF16),
        "act1s": ((3, 3, 2, PIX, HALF), BF16),
        "patch2": ((PIX, TAPS * BOT), BF16),
        "act2": ((2, PIX, HALF), BF16),
        "outb": ((4, 2, PIX, CH // 2), BF16),
        "outs": ((3, 6, 2, PIX, CH // 2), BF16),
        "patch": ((PIX, TAPS * CH), BF16),
        "part": ((8, LINE, HEADS), BF16),
        "partm": ((8, 8, HEADS), F32),
        "parts": ((TEAM, LINE, HEADS), BF16),
        "partsm": ((TEAM, 8, HEADS), F32),
        "preh": ((LINE, HEADS), F32),
        "acth": ((LINE, HEADS), BF16),
        "dyh": ((LINE, HEADS), F32),
        "dph": ((LINE, HEADS), BF16),
        "dpx": ((6, 2, LINE, HEADS), BF16),
        "dps": ((3, 6, PIX, HEADW), BF16),
        "grads": ((3, 4, PIX, CH), F32),
        "doutb": ((4, PIX, CH), BF16),
        "dout": ((4, PIX, CH), BF16),
        "du": ((PIX, WIDE), F32),
        "dpre3": ((PIX, WIDE), BF16),
        "half2": ((2, PIX, HALF), F32),
        "half2r": ((PIX, HALF), F32),
        "dy2": ((PIX, HALF), F32),
        "dp2": ((3, PIX, HALF), BF16),
        "half1": ((2, PIX, HALF), F32),
        "half1r": ((PIX, HALF), F32),
        "dy1": ((PIX, HALF), F32),
        "dp1": ((2, PIX, HALF), BF16),
        "dks": ((TAPS, CH // 2, HEADS), BF16),
        "dkr": ((TAPS, CH // 2, HEADS), BF16),
        "dku": ((TAPS, CH // 2, HEADS), BF16),
        "dproj": ((PROJ, HEADW), F32),
        "head_norm": ((8, HEADS), F32),
        "marks": ((8, LINE), jnp.int32),
        "values": ((16, LINE), F32),
        "proj": ((PROJ, HEADS), BF16),
        "dkg": ((shape.teams, TAPS, shape.unit, HEADS), BF16),
    }
    for name, count, width in (
        ("s1", 4, HALF), ("s2", 4, HALF), ("s3", 4, WIDE), ("t3", 4, WIDE), ("t2", 4, HALF), ("t1", 4, HALF),
        ("sh", 8, HEADS), ("th", 8, HEADS),
    ):
        table[name + "a"] = ((count, 8, width), F32)
        table[name + "b"] = ((planes, 8, width), F32)
    table["gma"] = ((8, 16 + PROJ, HEADW), F32)
    table["gmb"] = ((planes, 16 + PROJ, HEADW), F32)
    for index in range(3):
        rows, wide = shape.rows[index], shape.wide[index]
        if shape.inside:
            table[f"w{index}"] = ((planes, 4, rows, wide), BF16)
            table[f"dw{index}"] = ((planes, 4, rows, wide), BF16)
            table[f"ra{index}"] = ((2, planes, 2, rows // 2, wide), BF16)
            table[f"rb{index}"] = ((2, planes, rows // 2, wide), BF16)
            table[f"rc{index}"] = ((planes, rows, wide), BF16)
    return table


def fused(shape, names, used, *refs):
    env = dict(zip(names, refs))
    r_ = lambda name: env[name]
    s = lax.axis_index("section")
    d = lax.axis_index("dp")
    dp, planes, teams = shape.dp, shape.planes, shape.teams
    other = 1 - s
    plane, spot = d // 4, d % 4
    team, rank = d // TEAM, d % TEAM
    partner = (other, d)
    links = Links(r_("send"), r_("recv"), partner)

    gate = pltpu.get_barrier_semaphore()
    total = 2 * dp
    me = s * dp + d

    def greet(offset, carry):
        to = (me + offset) % total
        pl.semaphore_signal(gate, inc=1, device_id=(to // dp, to % dp), device_id_type=MESH)
        return carry

    lax.fori_loop(1, total, greet, 0)

    x = r_("x")
    for line in range(2):
        x[line * LINE:line * LINE + WS, :] = r_("small_feats")[line * WS:(line + 1) * WS, :]
        x[line * LINE + WS:(line + 1) * LINE, :] = r_("large_feats")[line * WL:(line + 1) * WL, :]
    marks, values, proj = r_("marks"), r_("values"), r_("proj")
    head_norm = r_("head_norm")
    for row, name in enumerate(("head_gain", "head_bias")):
        for part in range(HEADS // 128):
            head_norm[row:row + 1, part * 128:(part + 1) * 128] = r_(name)[part:part + 1, :]

    def own_line(section):
        small, large = slice(section * WS, (section + 1) * WS), slice(section * WL, (section + 1) * WL)
        for row, name in enumerate(("labels", "depth_valid", "normal_valid")):
            marks[row:row + 1, 0:WS] = r_("small_" + name)[:, small]
            marks[row:row + 1, WS:LINE] = r_("large_" + name)[:, large]
        for row, count, name in ((0, 1, "depth"), (8, 3, "normals")):
            values[row:row + count, 0:WS] = r_("small_" + name)[:, small]
            values[row:row + count, WS:LINE] = r_("large_" + name)[:, large]

    for section in range(2):
        pl.when(s == section)(functools.partial(own_line, section))
    proj[...] = jnp.zeros(proj.shape, BF16)
    for task, (row, name) in enumerate(((0, "seg_proj"), (DEPTH_ROW, "depth_proj"), (NORMAL_ROW, "normal_proj"))):
        matrix = r_(name)[...]
        proj[row:row + matrix.shape[0], task * HEADW:(task + 1) * HEADW] = matrix
    xh = r_("xh")
    xh_slot = links.slots()
    pltpu.make_async_copy(x.at[:, pl.ds(pl.multiple_of(s * WIDE, WIDE), WIDE)], xh, links.recv.at[xh_slot]).start()
    pl.semaphore_wait(gate, total - 1)

    def plane_sum(key, width_of):
        near = r_(key + "a")
        count = near.shape[0]
        own = spot if count == 4 else 4 * s + spot
        first = links.slots(count)
        for bits in range(1, count):
            to = flip(own, bits)
            device = (s, 4 * plane + to) if count == 4 else (to // 4, 4 * plane + to % 4)
            links.put(near.at[own], near.at[own], device, first + bits)

        def finish():
            for bits in range(1, count):
                links.landed(near.at[flip(own, bits)], first + bits)
            acc = near[0]
            for index in range(1, count):
                acc = acc + near[index]
            return acc

        return finish

    def line_sum(key, value):
        far = r_(key + "b")
        far[plane] = value
        first, out = links.slots(planes), links.outs(planes)

        def make(offset):
            to = (plane + offset) % planes
            return links.copy(far.at[plane], far.at[plane], (s, 4 * to + spot), out + offset, first + offset)

        several(planes - 1, lambda i: make(i + 1).start())
        links.open.append(lambda: several(planes - 1, lambda i: make(i + 1).wait_send()))

        def finish():
            several(planes - 1, lambda i: links.landed(far.at[0], first + i + 1))
            acc = far[0]
            for index in range(1, planes):
                acc = acc + far[index]
            return acc

        return finish

    def add_up(key):
        return line_sum(key, plane_sum(key, None)())()

    def own_slot(key):
        near = r_(key + "a")
        return near.at[spot if near.shape[0] == 4 else 4 * s + spot]

    def put_stats(key, rows, first, second=None):
        slot = own_slot(key)
        slot[...] = jnp.zeros(slot.shape, F32)
        for group in range(2):
            a = b = None
            for g, rng in seg_rows(rows):
                if g == group:
                    one, two = first(g, rng), second(g, rng)
                    one, two = jnp.sum(one, axis=0, keepdims=True), jnp.sum(two, axis=0, keepdims=True)
                    a, b = (one, two) if a is None else (a + one, b + two)
            slot[2 * group:2 * group + 1, :] = a
            slot[2 * group + 1:2 * group + 2, :] = b

    counts = (2.0 * dp * WS, 2.0 * dp * WL)

    def moments(sums):
        means, invs = [], []
        for group in range(2):
            mean = sums[2 * group:2 * group + 1, :] / counts[group]
            var = sums[2 * group + 1:2 * group + 2, :] / counts[group] - mean * mean
            means.append(mean)
            invs.append(lax.rsqrt(var + EPS))
        return means, invs

    gathers = []
    if shape.inside:
        shards = (
            r_("reduce_w").at[:, pl.ds(pl.multiple_of(s * HALF, HALF), HALF)],
            r_("dilated_w").at[:, pl.ds(pl.multiple_of(s * HALF, HALF), HALF)],
            r_("expand_w").at[:, pl.ds(pl.multiple_of(s * WIDE, WIDE), WIDE)],
        )
        near_x, near_y, corner = flip(spot, 1), flip(spot, 2), flip(spot, 3)
        at_x, at_y = (s, 4 * plane + near_x), (s, 4 * plane + near_y)

        def gather(index):
            rows, wide = shape.rows[index], shape.wide[index]
            buf = r_(f"w{index}")
            cut = rows // 2
            first, out = links.slots(planes), links.outs(planes)
            mine = pltpu.make_async_copy(shards[index], buf.at[plane, spot], links.recv.at[first])
            mine.start()

            def make(offset):
                to = (plane + offset) % planes
                return links.copy(shards[index], buf.at[plane, spot], (s, 4 * to + spot), out + offset, first + offset)

            several(planes - 1, lambda i: make(i + 1).start())
            links.open.append(lambda: several(planes - 1, lambda i: make(i + 1).wait_send()))
            up, low = pl.ds(0, cut), pl.ds(cut, cut)
            slot = links.slots(6)
            yield
            mine.wait()
            several(planes - 1, lambda i: links.landed(buf.at[0, 0], first + i + 1))
            links.put(buf.at[:, spot, up], buf.at[:, spot, up], at_x, slot)
            links.put(buf.at[:, spot, low], buf.at[:, spot, low], at_y, slot + 1)
            links.put(buf.at[:, spot, up], buf.at[:, spot, up], at_y, slot + 2)
            links.put(buf.at[:, spot, low], buf.at[:, spot, low], at_x, slot + 3)
            yield
            links.landed(buf.at[:, near_x, up], slot)
            links.put(buf.at[:, near_x, up], buf.at[:, near_x, up], at_y, slot + 4)
            links.landed(buf.at[:, near_y, low], slot + 1)
            links.put(buf.at[:, near_y, low], buf.at[:, near_y, low], at_x, slot + 5)
            yield
            links.landed(buf.at[:, near_y, up], slot + 2)
            links.landed(buf.at[:, near_x, low], slot + 3)
            links.landed(buf.at[:, corner, up], slot + 4)
            links.landed(buf.at[:, corner, low], slot + 5)
            yield

        gathers = [gather(index) for index in range(3)]
        for one in gathers:
            next(one)
        weights = [r_(f"w{index}") for index in range(3)]
    else:
        weights = [r_("reduce_w"), r_("dilated_w"), r_("expand_w")]

    def gather_on(index):
        if shape.inside:
            next(gathers[index])

    kernel = r_("kernel")
    unit, halves = shape.unit, shape.units_half
    share = 2 * halves
    kernel_slot = links.slots(TAPS * halves)
    kernel_out = links.outs(TAPS * teams)

    def unit_at(index):
        number = TAPS * d + index
        tap, chunk = number // dp, number % dp
        inner = chunk % share
        return inner // halves == s, chunk // share, tap, inner % halves

    def kernel_copy(index, to_team):
        sends, to_rank, tap, place = unit_at(index)
        src = r_("head_w").at[index]
        dst = kernel.at[tap, s, pl.ds(pl.multiple_of(place * unit, unit), unit)]
        to = to_team * TEAM + to_rank
        slot = kernel_slot + tap * halves + place
        to_core = jnp.where(to == d, other, s)
        remote = lambda: links.copy(src, dst, (to_core, to), kernel_out + index * teams + to_team, slot)
        local = lambda: pltpu.make_async_copy(src, dst, links.recv.at[slot])
        return sends, to == d, remote, local

    def kernel_start(index, to_team):
        sends, mine, remote, local = kernel_copy(index, to_team)
        pl.when(sends & mine)(lambda: local().start())
        pl.when(sends & jnp.logical_not(mine))(lambda: remote().start())

    def kernel_done(index, to_team):
        sends, mine, remote, _ = kernel_copy(index, to_team)
        pl.when(sends & jnp.logical_not(mine))(lambda: remote().wait_send())

    def kernel_send():
        lax.fori_loop(0, TAPS * teams, lambda i, c: (kernel_start(i // teams, i % teams), c)[1], 0)

    links.open.append(lambda: lax.fori_loop(0, TAPS * teams, lambda i, c: (kernel_done(i // teams, i % teams), c)[1], 0))

    def same_image(block, tap_row):
        near = block + (tap_row - 1)
        inside = (near >= 0) & (near < dp)
        return [inside & ((2 * near + 2 * height) // height == (2 * block + 2 * height) // height) for height in HEIGHTS]

    def row_mask(block, tap_row, rows=PIX):
        small, large = [flag.astype(F32) for flag in same_image(block, tap_row)]
        return jnp.where(position(rows) < WS, small, large)

    def own_part(name, width):
        return r_(name)[0:1, pl.ds(pl.multiple_of(s * width, width), width)]

    norm1 = own_part("reduce_gain", HALF), own_part("reduce_bias", HALF)
    norm2 = own_part("dilated_gain", HALF), own_part("dilated_bias", HALF)
    norm3 = own_part("expand_gain", WIDE), own_part("expand_bias", WIDE)
    pre1, pre2, pre3 = r_("pre1"), r_("pre2"), r_("pre3")
    act1, act2 = r_("act1"), r_("act2")
    squares = lambda ref: (lambda g, rng: ref[rng, :], lambda g, rng: ref[rng, :] * ref[rng, :])

    gather_on(0)
    gather_on(0)
    gather_on(1)
    kernel_send()
    gather_on(0)
    pre1[...] = mm(x[...], take_rows(weights[0], 0, C))
    back_slot = links.slots()
    half_planes = planes // 2

    def rows_half(section):
        if shape.inside:
            return weights[0].at[pl.ds(pl.multiple_of(section * half_planes, half_planes), half_planes)]
        return weights[0].at[pl.ds(pl.multiple_of(section * WIDE, WIDE), WIDE)]

    links.put(rows_half(other), r_("wback"), partner, back_slot)
    put_stats("s1", 2, *squares(pre1))
    gather_on(1)
    gather_on(2)
    mean1, inv1 = moments(add_up("s1"))
    gain, bias = norm1
    for group, rng in seg_rows(2):
        hat = (pre1[rng, :] - mean1[group]) * inv1[group]
        pre1[rng, :] = hat
        act1[1, s, rng, :] = silu(hat * gain + bias).astype(BF16)
    slot = links.slots(5)
    above, below = jnp.maximum(d - 1, 0), jnp.minimum(d + 1, dp - 1)
    has_above, has_below = d > 0, d < dp - 1
    links.put(act1.at[1, s], act1.at[2, s], (s, above), slot + 1 + s, has_above)
    links.put(act1.at[1, s], act1.at[0, s], (s, below), slot + 3 + s, has_below)
    links.put(act1.at[1, s], act1.at[1, s], partner, slot)

    @pl.when(jnp.logical_not(has_above))
    def _():
        act1[0] = jnp.zeros(act1.shape[1:], BF16)

    @pl.when(jnp.logical_not(has_below))
    def _():
        act1[2] = jnp.zeros(act1.shape[1:], BF16)

    act1s, patch2 = r_("act1s"), r_("patch2")
    gather_on(2)

    def spread_rows(tap_row, half):
        value = act1[tap_row, half].astype(F32)
        if tap_row != 1 and shape.borders:
            value = value * row_mask(d, tap_row)
        for tap_col in range(3):
            piece = sideways(value, tap_col).astype(BF16)
            at = (3 * tap_row + tap_col) * BOT + half * HALF
            act1s[tap_col, tap_row, half] = piece
            patch2[:, at:at + HALF] = piece

    links.landed(act1.at[1, other], slot)
    for half in range(2):
        spread_rows(1, half)
    links.landed(act1.at[2, s], slot + 1 + s, has_below)
    links.put(act1.at[2, s], act1.at[2, s], partner, slot + 1 + s, has_below)
    links.landed(act1.at[0, s], slot + 3 + s, has_above)
    links.put(act1.at[0, s], act1.at[0, s], partner, slot + 3 + s, has_above)
    links.landed(act1.at[2, other], slot + 1 + other, has_below)
    for half in range(2):
        spread_rows(2, half)
    links.landed(act1.at[0, other], slot + 3 + other, has_above)
    for half in range(2):
        spread_rows(0, half)
    gather_on(1)
    pre2[...] = mm(patch2[...], take_rows(weights[1], 0, TAPS * BOT))
    put_stats("s2", 2, *squares(pre2))
    mean2, inv2 = moments(add_up("s2"))
    gain, bias = norm2
    for group, rng in seg_rows(2):
        hat = (pre2[rng, :] - mean2[group]) * inv2[group]
        pre2[rng, :] = hat
        act2[s, rng, :] = silu(hat * gain + bias).astype(BF16)
    slot = links.slots()
    links.put(act2.at[s], act2.at[s], partner, slot)
    gather_on(2)
    links.landed(act2.at[other], slot)
    pre3[...] = mm(act2[0], take_rows(weights[2], 0, HALF)) + mm(act2[1], take_rows(weights[2], HALF, HALF))
    put_stats("s3", 2, *squares(pre3))
    mean3, inv3 = moments(add_up("s3"))
    links.landed(xh, xh_slot)
    gain, bias = norm3
    outb = r_("outb")
    for group, rng in seg_rows(2):
        hat = (pre3[rng, :] - mean3[group]) * inv3[group]
        pre3[rng, :] = hat
        value = silu(hat * gain + bias + xh[rng, :].astype(F32)).astype(BF16)
        for part in range(4):
            for half in range(2):
                at = part * CH + half * (CH // 2)
                outb[part, half, rng, :] = value[:, at:at + CH // 2]
        start, length = SEGMENTS[group]
        line = rng.start // LINE
        whole = r_(("small_out_o", "large_out_o")[group])
        whole[line * length:(line + 1) * length, pl.ds(pl.multiple_of(s * WIDE, WIDE), WIDE)] = value

    outs = r_("outs")
    seat = rank // 4
    slot = links.slots(6)
    for part in range(4):
        to_rank = 4 * s + part
        src = outb.at[part]
        chip = team * TEAM + to_rank
        links.put_or_keep(src, outs.at[1, rank % 4 + 1], (seat, chip), slot + rank % 4 + 1, (seat == s) & (part == rank % 4))
    out_slot = links.slots(2)
    out_parts = [r_(name).at[:, pl.ds(pl.multiple_of(s * WIDE, WIDE), WIDE)] for name in ("small_out_o", "large_out_o")]
    for index, out_part in enumerate(out_parts):
        links.put(out_part, out_part, partner, out_slot + index)
    has_low = (s == 1) | (team > 0)
    has_high = (s == 0) | (team < teams - 1)

    @pl.when(jnp.logical_not(has_low))
    def _():
        outs[1, 0] = jnp.zeros((2, PIX, CH // 2), BF16)

    @pl.when(jnp.logical_not(has_high))
    def _():
        outs[1, 5] = jnp.zeros((2, PIX, CH // 2), BF16)

    near_block, near_border = 4 - 3 * s, 5 * s
    far_block, far_border = 1 + 3 * s, 5 - 5 * s
    far_chip = (other, jnp.clip(d + TEAM * (2 * s - 1), 0, dp - 1))
    has_far = (has_low & (s == 0)) | (has_high & (s == 1))
    for index in range(1, 5):
        links.landed(outs.at[1, index], slot + index)
    links.put(outs.at[1, near_block], outs.at[1, near_border], partner, slot + near_border)
    links.put(outs.at[1, far_block], outs.at[1, far_border], far_chip, slot + far_border, has_far)

    swap_slot = links.slots()
    several(TAPS * halves, lambda i: links.landed(kernel.at[0, 0, pl.ds(0, unit)], kernel_slot + i))
    links.put(kernel.at[:, s], kernel.at[:, s], partner, swap_slot)

    def widen(index, carry):
        for half in range(2):
            value = outs[1, index, half].astype(F32)
            outs[0, index, half] = sideways(value, 0).astype(BF16)
            outs[2, index, half] = sideways(value, 2).astype(BF16)
        return carry

    lax.fori_loop(1, 5, widen, 0)
    links.landed(kernel.at[:, other], swap_slot)

    first_block = team * TEAM + 4 * s
    patch, part, partm = r_("patch"), r_("part"), r_("partm")
    parts, partsm = r_("parts"), r_("partsm")
    part_slot = links.slots(2 * TEAM)

    def head_block(index):
        for tap_row in range(3):
            for tap_col in range(3):
                for half in range(2):
                    piece = outs[tap_col, index + tap_row, half]
                    if tap_row != 1 and shape.borders:
                        piece = piece * row_mask(first_block + index, tap_row).astype(BF16)
                    at = (3 * tap_row + tap_col) * CH + half * (CH // 2)
                    patch[:, at:at + CH // 2] = piece
        value = mm(patch[...], kernel[...].reshape(TAPS * CH, HEADS))
        for line in range(2):
            number = 2 * index + line
            for group, (start, length) in enumerate(SEGMENTS):
                rows = value[line * LINE + start:line * LINE + start + length, :]
                middle = jnp.mean(rows, axis=0, keepdims=True)
                partm[number, group:group + 1, :] = middle
                part[number, start:start + length, :] = (rows - middle).astype(BF16)
            chip = team * TEAM + 4 * s + index
            mine = (4 * s + index == rank) & (s == line)
            links.put_or_keep(part.at[number], parts.at[rank], (line, chip), part_slot + rank, mine)
            links.put_or_keep(partm.at[number], partsm.at[rank], (line, chip), part_slot + TEAM + rank, mine)

    head_block(1)
    head_block(2)
    links.landed(outs.at[1, 0], slot, has_low)
    links.landed(outs.at[1, 5], slot + 5, has_high)
    widen(0, 0)
    widen(5, 0)
    head_block(0)
    head_block(3)

    for index in range(TEAM):
        links.landed(parts.at[index], part_slot + index)
        links.landed(partsm.at[index], part_slot + TEAM + index)
    preh, acth, dyh = r_("preh"), r_("acth"), r_("dyh")
    for group, (start, length) in enumerate(SEGMENTS):
        rng = slice(start, start + length)
        acc = sum(parts[index, rng, :].astype(F32) for index in range(TEAM))
        acc = acc + sum(partsm[index, group:group + 1, :] for index in range(TEAM))
        preh[rng, :] = acc

    labels, depth, normals = marks[0:1, :], values[0:1, :], values[8:11, :]
    seg_keep = (labels >= 0).astype(F32)
    depth_keep, normal_keep = marks[1:2, :].astype(F32), marks[2:3, :].astype(F32)
    lane = lax.broadcasted_iota(jnp.int32, (1, LINE), 1)
    small_lane = lane < WS
    put_stats("sh", 1, *squares(preh))
    slot_ref = own_slot("sh")
    tally = jnp.zeros((1, LINE), F32)
    for number, keep in enumerate((seg_keep, depth_keep, normal_keep)):
        for group in range(2):
            count = jnp.sum(jnp.where(small_lane == (group == 0), keep, 0.0), axis=1, keepdims=True)
            tally = tally + jnp.where(lane == 2 * number + group, count, 0.0)
    slot_ref[4:5, 0:LINE] = tally
    sums = add_up("sh")
    meanh, invh = moments(sums)
    tally = sums[4:5, 0:LINE]

    def pixel_count(number):
        picked = [jnp.sum(jnp.where(lane == 2 * number + group, tally, 0.0), axis=1, keepdims=True) for group in range(2)]
        return jnp.maximum(jnp.where(small_lane, picked[0], picked[1]), 1.0)

    gain, bias = head_norm[0:1, :], head_norm[1:2, :]
    for group, rng in seg_rows(1):
        hat = (preh[rng, :] - meanh[group]) * invh[group]
        preh[rng, :] = hat
        acth[rng, :] = silu(hat * gain + bias).astype(BF16)

    scores = mm(proj[...], acth[...], NT)
    row = lax.broadcasted_iota(jnp.int32, (16, LINE), 0)
    logits = jnp.where(row < NCLS, scores[0:16, :], -1e30)
    top = jnp.max(logits, axis=0, keepdims=True)
    power = jnp.where(row < NCLS, jnp.exp(logits - top), 0.0)
    soft = power / jnp.sum(power, axis=0, keepdims=True)
    onehot = (row == labels).astype(F32)
    d_logits = (soft - onehot) * (seg_keep / pixel_count(0))
    gap = scores[DEPTH_ROW:DEPTH_ROW + 1, :] - depth
    d_depth = depth_keep / pixel_count(1) * gap * lax.rsqrt(gap * gap + 1.0)
    guess = scores[NORMAL_ROW:NORMAL_ROW + 3, :]
    inverse = lax.rsqrt(jnp.sum(guess * guess, axis=0, keepdims=True) + 1.0)
    along = jnp.sum(guess * normals, axis=0, keepdims=True)
    weight = normal_keep / pixel_count(2)
    d_guess = r_("dscore")
    d_guess[...] = jnp.zeros(d_guess.shape, F32)
    d_guess[0:16, :] = d_logits
    d_guess[DEPTH_ROW:DEPTH_ROW + 1, :] = d_depth
    d_guess[NORMAL_ROW:NORMAL_ROW + 3, :] = -weight * (normals * inverse - along * (inverse * inverse * inverse) * guess)
    d_scores = d_guess[...]
    high = d_scores.astype(BF16)
    low = (d_scores - high.astype(F32)).astype(BF16)
    d_act = mm(high, proj[...], TN) + mm(low, proj[...], TN)
    value = mm(high, acth[...]) + mm(low, acth[...])
    d_proj = r_("dproj")
    d_proj[0:16, :] = value[0:16, 0:HEADW]
    d_proj[16:24, :] = value[16:24, HEADW:2 * HEADW]
    d_proj[24:32, :] = value[24:32, 2 * HEADW:]
    for group, rng in seg_rows(1):
        dyh[rng, :] = d_act[rng, :] * slope(preh[rng, :] * gain + bias)
    put_stats("th", 1, lambda g, rng: dyh[rng, :], lambda g, rng: dyh[rng, :] * preh[rng, :])
    sums = add_up("th")
    r_("head_vec_o")[...] = sums
    dph, dpx = r_("dph"), r_("dpx")
    for group, rng in seg_rows(1):
        first, second = sums[2 * group:2 * group + 1, :], sums[2 * group + 1:2 * group + 2, :]
        value = dyh[rng, :] - first / counts[group] - preh[rng, :] * (second / counts[group])
        dph[rng, :] = (gain * invh[group] * value).astype(BF16)

    slot = links.slots(12)
    place = rank % 4 + 1
    for step in range(TEAM):
        chip = team * TEAM + flip(rank, step)
        if step == 0:
            links.put_or_keep(dph, dpx.at[place, s], (seat, chip), slot + 2 * place + s, seat == s)
        else:
            links.put(dph, dpx.at[place, s], (seat, chip), slot + 2 * place + s)

    @pl.when(jnp.logical_not(has_low))
    def _():
        dpx[0] = jnp.zeros((2, LINE, HEADS), BF16)

    @pl.when(jnp.logical_not(has_high))
    def _():
        dpx[5] = jnp.zeros((2, LINE, HEADS), BF16)

    for index in range(2, 10):
        links.landed(dpx.at[index // 2, index % 2], slot + index)
    links.put(dpx.at[near_block], dpx.at[near_border], partner, slot + 2 * near_border)
    links.put(dpx.at[far_block], dpx.at[far_border], far_chip, slot + 2 * far_border, has_far)
    links.landed(dpx.at[0], slot, has_low)
    links.landed(dpx.at[5], slot + 10, has_high)

    dks, dkr, dku, dkg = r_("dks"), r_("dkr"), r_("dku"), r_("dkg")

    def tap_grad(tap, half):
        tap_row, tap_col = tap // 3, tap % 3
        acc = None
        for index in range(4):
            left = outs[tap_col, index + tap_row, half]
            right = dpx[index + 1].reshape(PIX, HEADS)
            if shape.borders:
                right = right * row_mask(first_block + index, tap_row).astype(BF16)
            term = mm(left, right, TN)
            acc = term if acc is None else acc + term
        return acc

    def their_tap(tap, carry):
        dks[tap] = tap_grad(tap, other).astype(BF16)
        return carry

    lax.fori_loop(0, TAPS, their_tap, 0)
    swap_slot = links.slots()
    links.put(dks, dkr, partner, swap_slot)

    dps, grads = r_("dps"), r_("grads")
    for task in range(3):
        cols = slice(task * HEADW, (task + 1) * HEADW)

        def spread(index, carry):
            piece = dpx[index, :, :, cols].reshape(PIX, HEADW)
            value = piece.astype(F32)
            dps[1, index] = piece
            dps[0, index] = sideways(value, 0).astype(BF16)
            dps[2, index] = sideways(value, 2).astype(BF16)
            return carry

        lax.fori_loop(0, 6, spread, 0)

        def pull(index, carry):
            acc = None
            for tap_row in range(3):
                for tap_col in range(3):
                    piece = dps[tap_col, index + tap_row]
                    if tap_row != 1 and shape.borders:
                        piece = piece * row_mask(first_block + index, tap_row).astype(BF16)
                    tap = 8 - (3 * tap_row + tap_col)
                    term = mm(piece, kernel[tap, :, :, cols].reshape(CH, HEADW), NT)
                    acc = term if acc is None else acc + term
            grads[task, index] = acc
            return carry

        lax.fori_loop(0, 4, pull, 0)

    pairs = [(i, j) for i in range(3) for j in range(i, 3)]

    def dots(index, sums):
        sums = list(sums)
        for group, rng in seg_rows(2):
            block = [grads[task, index, rng, :] for task in range(3)]
            for number, (i, j) in enumerate(pairs):
                sums[6 * group + number] += jnp.sum(block[i] * block[j], axis=0, keepdims=True)
        return tuple(sums)

    sums = lax.fori_loop(0, 4, dots, (jnp.zeros((1, CH), F32),) * (2 * len(pairs)))
    slot_ref = own_slot("gm")
    slot_ref[0:16, :] = jnp.zeros((16, HEADW), F32)
    for number, total_row in enumerate(sums):
        slot_ref[number:number + 1, :] = total_row
    slot_ref[16:, :] = d_proj[...]
    near_done = plane_sum("gm", None)

    def my_tap(tap, carry):
        dku[tap] = tap_grad(tap, s).astype(BF16)
        return carry

    lax.fori_loop(0, TAPS, my_tap, 0)
    links.landed(dkr, swap_slot)

    def both(tap, carry):
        dku[tap] = (dku[tap].astype(F32) + dkr[tap].astype(F32)).astype(BF16)
        return carry

    lax.fori_loop(0, TAPS, both, 0)

    grad_slot = links.slots(teams * TAPS)
    grad_out = links.outs(TAPS * halves)

    def grad_copy(number):
        tap, place = number // halves, number % halves
        chunk = rank * share + s * halves + place
        overall = tap * dp + chunk
        owner, index = overall // TAPS, overall % TAPS
        src = dku.at[tap, pl.ds(pl.multiple_of(place * unit, unit), unit)]
        dst = dkg.at[team, index]
        at = grad_slot + team * TAPS + index
        to_core = jnp.where(owner == d, other, s)
        remote = lambda: links.copy(src, dst, (to_core, owner), grad_out + number, at)
        local = lambda: pltpu.make_async_copy(src, dst, links.recv.at[at])
        return owner == d, remote, local

    def grad_start(number):
        mine, remote, local = grad_copy(number)
        pl.when(mine)(lambda: local().start())
        pl.when(jnp.logical_not(mine))(lambda: remote().start())

    def grad_done(number):
        mine, remote, _ = grad_copy(number)
        pl.when(jnp.logical_not(mine))(lambda: remote().wait_send())

    lax.fori_loop(0, TAPS * halves, lambda i, c: (grad_start(i), c)[1], 0)
    links.open.append(lambda: lax.fori_loop(0, TAPS * halves, lambda i, c: (grad_done(i), c)[1], 0))

    far_done = line_sum("gm", near_done())
    gram_rows = far_done()
    r_("proj_o")[...] = gram_rows[16:, :]
    dot_of = jnp.sum(gram_rows[0:16, :], axis=1, keepdims=True)
    gram = {
        pair: jnp.where(lane == 0, dot_of[k:k + 1, :], dot_of[6 + k:7 + k, :]) for k, pair in enumerate(pairs)
    }
    alphas = jacobi_weights(gram)
    alphas = [[alpha[:, group:group + 1] for alpha in alphas] for group in range(2)]

    doutb, dout = r_("doutb"), r_("dout")
    slot = links.slots(4)
    for index in range(4):
        for group, rng in seg_rows(2):
            aligned = sum(alphas[group][task] * grads[task, index, rng, :] for task in range(3))
            doutb[index, rng, :] = aligned.astype(BF16)
        chip = team * TEAM + 4 * s + index
        links.put_or_keep(
            doutb.at[index], dout.at[rank % 4], (seat, chip), slot + rank % 4, (seat == s) & (rank % 4 == index)
        )

    for index in range(4):
        links.landed(dout.at[index], slot + index)
    du, dpre3 = r_("du"), r_("dpre3")
    gain, bias = norm3
    for group, rng in seg_rows(2):
        at = slope(pre3[rng, :] * gain + bias + xh[rng, :].astype(F32))
        for part_index in range(4):
            cols = slice(part_index * CH, (part_index + 1) * CH)
            du[rng, cols] = dout[part_index, rng, :].astype(F32) * at[:, cols]
    vec = r_("vec_o")
    with_hat = lambda dy, hat: (lambda g, rng: dy[rng, :], lambda g, rng: dy[rng, :] * hat[rng, :])
    put_stats("t3", 2, *with_hat(du, pre3))
    sums = add_up("t3")
    vec[s, 0:1, :] = sums[1:2, :] + sums[3:4, :]
    vec[s, 1:2, :] = sums[0:1, :] + sums[2:3, :]

    def norm_back(sums, group, rng, dy, hat, scale):
        first, second = sums[2 * group:2 * group + 1, :], sums[2 * group + 1:2 * group + 2, :]
        return scale * (dy[rng, :] - first / counts[group] - hat[rng, :] * (second / counts[group]))

    for group, rng in seg_rows(2):
        dpre3[rng, :] = norm_back(sums, group, rng, du, pre3, gain * inv3[group]).astype(BF16)
    half2, half2r = r_("half2"), r_("half2r")
    value = mm(dpre3[...], take_rows(weights[2], 0, BOT), NT)
    half2[0], half2[1] = value[:, :HALF], value[:, HALF:]
    slot = links.slots()
    links.put(half2.at[other], half2r, partner, slot)

    def scatter(index):
        rows, wide = shape.rows[index], shape.wide[index]
        cut = rows // 2
        up, low = pl.ds(0, cut), pl.ds(cut, cut)
        buf = r_(f"dw{index}")
        ra, rb, rc = r_(f"ra{index}"), r_(f"rb{index}"), r_(f"rc{index}")
        slot = links.slots(6)
        links.put(buf.at[:, near_y, up], ra.at[0, :, 0], at_y, slot)
        links.put(buf.at[:, corner, up], ra.at[0, :, 1], at_y, slot + 1)
        links.put(buf.at[:, near_x, low], ra.at[1, :, 0], at_x, slot + 2)
        links.put(buf.at[:, corner, low], ra.at[1, :, 1], at_x, slot + 3)
        yield

        def add(at, part, extra):
            total = buf[:, at, part].astype(F32) + extra.astype(F32)
            buf[:, at, part] = total.astype(BF16)

        links.landed(ra.at[0, :, 1], slot + 1)
        add(near_x, up, ra[0, :, 1])
        links.put(buf.at[:, near_x, up], rb.at[0], at_x, slot + 4)
        links.landed(ra.at[1, :, 1], slot + 3)
        add(near_y, low, ra[1, :, 1])
        links.put(buf.at[:, near_y, low], rb.at[1], at_y, slot + 5)
        yield
        links.landed(ra.at[0, :, 0], slot)
        links.landed(ra.at[1, :, 0], slot + 2)
        links.landed(rb.at[0], slot + 4)
        add(spot, up, ra[0, :, 0].astype(F32) + rb[0].astype(F32))
        links.landed(rb.at[1], slot + 5)
        add(spot, low, ra[1, :, 0].astype(F32) + rb[1].astype(F32))
        first, out = links.slots(planes), links.outs(planes)

        def make(offset):
            to = (plane + offset) % planes
            return links.copy(buf.at[to, spot], rc.at[plane], (s, 4 * to + spot), out + offset, first + offset)

        several(planes - 1, lambda i: make(i + 1).start())
        links.open.append(lambda: several(planes - 1, lambda i: make(i + 1).wait_send()))
        rc[plane] = buf[plane, spot]
        yield
        several(planes - 1, lambda i: links.landed(rc.at[0], first + i + 1))
        acc = rc[0].astype(F32)
        for number in range(1, planes):
            acc = acc + rc[number].astype(F32)
        result = r_(f"dw{index}_o")
        mine = pl.ds(pl.multiple_of(s * wide, wide), wide)
        result[:, mine] = acc.astype(BF16)
        at = links.slots()
        links.put(result.at[:, mine], result.at[:, mine], partner, at)
        yield
        links.landed(result.at[:, mine], at)
        yield

    def advance(one):
        if one is not None:
            next(one)

    def reduced(index):
        if not shape.inside:
            return None
        one = scatter(index)
        next(one)
        return one

    grad_of = lambda index: r_(f"dw{index}") if shape.inside else r_(f"dw{index}_o")
    for half in range(2):
        put_rows(grad_of(2), half * HALF, mm(act2[half], dpre3[...], TN).astype(BF16))
    third = reduced(2)

    links.landed(half2r, slot)
    dy2, dp2 = r_("dy2"), r_("dp2")
    gain, bias = norm2
    for group, rng in seg_rows(2):
        value = half2[s, rng, :] + half2r[rng, :]
        dy2[rng, :] = value * slope(pre2[rng, :] * gain + bias)
    put_stats("t2", 2, *with_hat(dy2, pre2))
    advance(third)
    sums = add_up("t2")
    vec[s, 2:3, 0:HALF] = sums[1:2, :] + sums[3:4, :]
    vec[s, 2:3, HALF:2 * HALF] = sums[0:1, :] + sums[2:3, :]
    for group, rng in seg_rows(2):
        dp2[1, rng, :] = norm_back(sums, group, rng, dy2, pre2, gain * inv2[group]).astype(BF16)
    slot = links.slots(2)
    links.put(dp2.at[1], dp2.at[2], (s, above), slot, has_above)
    links.put(dp2.at[1], dp2.at[0], (s, below), slot + 1, has_below)

    @pl.when(jnp.logical_not(has_above))
    def _():
        dp2[0] = jnp.zeros((PIX, HALF), BF16)

    @pl.when(jnp.logical_not(has_below))
    def _():
        dp2[2] = jnp.zeros((PIX, HALF), BF16)

    for tap in range(TAPS):
        for half in range(2):
            at = tap * BOT + half * HALF
            put_rows(grad_of(1), at, mm(act1s[tap % 3, tap // 3, half], dp2[1], TN).astype(BF16))
    second = reduced(1)
    advance(third)
    links.landed(dp2.at[2], slot, has_below)
    links.landed(dp2.at[0], slot + 1, has_above)
    acc = None
    for tap_row in range(3):
        value = dp2[tap_row].astype(F32)
        if tap_row != 1 and shape.borders:
            value = value * row_mask(d, tap_row)
        for tap_col in range(3):
            tap = 8 - (3 * tap_row + tap_col)
            term = mm(sideways(value, tap_col).astype(BF16), take_rows(weights[1], tap * BOT, BOT), NT)
            acc = term if acc is None else acc + term
    half1, half1r = r_("half1"), r_("half1r")
    half1[0], half1[1] = acc[:, :HALF], acc[:, HALF:]
    slot = links.slots()
    links.put(half1.at[other], half1r, partner, slot)
    advance(second)
    links.landed(half1r, slot)
    dy1, dp1 = r_("dy1"), r_("dp1")
    gain, bias = norm1
    for group, rng in seg_rows(2):
        value = half1[s, rng, :] + half1r[rng, :]
        dy1[rng, :] = value * slope(pre1[rng, :] * gain + bias)
    put_stats("t1", 2, *with_hat(dy1, pre1))
    sums = add_up("t1")
    vec[s, 2:3, 2 * HALF:3 * HALF] = sums[1:2, :] + sums[3:4, :]
    vec[s, 2:3, 3 * HALF:4 * HALF] = sums[0:1, :] + sums[2:3, :]
    vec[s, 3:8, :] = jnp.zeros((5, WIDE), F32)
    vec_slot = links.slots()
    links.put(vec.at[s], vec.at[s], partner, vec_slot)
    for group, rng in seg_rows(2):
        dp1[s, rng, :] = norm_back(sums, group, rng, dy1, pre1, gain * inv1[group]).astype(BF16)
    slot = links.slots()
    links.put(dp1.at[s], dp1.at[s], partner, slot)
    for part_index in range(4):
        cols = slice(part_index * BOT, (part_index + 1) * BOT)
        put_rows(grad_of(0), part_index * BOT, mm(x[:, cols], dp1[s], TN).astype(BF16))
    first = reduced(0)
    advance(second)
    advance(third)

    links.landed(r_("wback"), back_slot)
    links.landed(dp1.at[other], slot)
    value = mm(dp1[s], rows_half(s)[...].reshape(WIDE, HALF), NT)
    value = value + mm(dp1[other], r_("wback")[...].reshape(WIDE, HALF), NT) + du[...]
    for line in range(2):
        r_("small_grad_o")[line * WS:(line + 1) * WS, :] = value[line * LINE:line * LINE + WS, :]
        r_("large_grad_o")[line * WL:(line + 1) * WL, :] = value[line * LINE + WS:(line + 1) * LINE, :]
    advance(first)
    advance(second)
    advance(first)

    result = r_("dk_o")
    done_slot, done_out = links.slots(TAPS), links.outs(TAPS)

    def finish_unit(index):
        mine, _, _, _ = unit_at(index)
        final = lambda: links.copy(result.at[index], result.at[index], partner, done_out + index, done_slot + index)

        @pl.when(mine)
        def _():
            several(teams, lambda t: links.landed(dkg.at[0, 0], grad_slot + t * TAPS + index))
            acc = dkg[0, index].astype(F32)
            for number in range(1, teams):
                acc = acc + dkg[number, index].astype(F32)
            result[index] = acc.astype(BF16)
            final().start()

        return mine, final

    lax.fori_loop(0, TAPS, lambda i, c: (finish_unit(i), c)[1], 0)

    def finished(index):
        mine, _, _, _ = unit_at(index)
        final = links.copy(result.at[index], result.at[index], partner, done_out + index, done_slot + index)
        pl.when(mine)(lambda: final.wait_send())
        pl.when(jnp.logical_not(mine))(lambda: links.landed(result.at[index], done_slot + index))

    advance(first)
    advance(first)
    advance(second)
    advance(third)
    lax.fori_loop(0, TAPS, lambda i, c: (finished(i), c)[1], 0)
    links.landed(vec.at[other], vec_slot)
    for index, out_part in enumerate(out_parts):
        links.landed(out_part, out_slot + index)
    links.close()
    used["send"], used["recv"] = links.used_send, links.used_recv


def body(
    reduce_weight,
    dilated_weight,
    expand_weight,
    reduce_gain,
    reduce_bias,
    dilated_gain,
    dilated_bias,
    expand_gain,
    expand_bias,
    head_conv,
    head_gain,
    head_bias,
    seg_proj,
    depth_proj,
    normal_proj,
    small_feats,
    small_labels,
    small_depth,
    small_normals,
    small_depth_valid,
    small_normal_valid,
    large_feats,
    large_labels,
    large_depth,
    large_normals,
    large_depth_valid,
    large_normal_valid,
):
    dp = lax.axis_size("dp")
    section = lax.axis_index("section")
    assert small_feats.shape[0] == 2 * WS and large_feats.shape[0] == 2 * WL
    shape = Shapes(dp)

    if not shape.inside:
        def whole(shard, wide):
            mine = lax.dynamic_slice_in_dim(shard, section * wide, wide, 1)
            return lax.all_gather(mine, "dp", axis=0, tiled=True)

        reduce_weight = whole(reduce_weight, HALF)
        dilated_weight = whole(dilated_weight, HALF)
        expand_weight = whole(expand_weight, WIDE)

    vmem = pl.BlockSpec(memory_space=pltpu.VMEM)
    anywhere = pl.BlockSpec(memory_space=pl.ANY)
    flat = lambda value: value.reshape(1, -1)
    inputs = {
        "reduce_w": reduce_weight,
        "dilated_w": dilated_weight,
        "expand_w": expand_weight,
        "head_w": head_conv.reshape(TAPS, shape.unit, HEADS),
        "reduce_gain": flat(reduce_gain),
        "reduce_bias": flat(reduce_bias),
        "dilated_gain": flat(dilated_gain),
        "dilated_bias": flat(dilated_bias),
        "expand_gain": flat(expand_gain),
        "expand_bias": flat(expand_bias),
        "head_gain": head_gain.reshape(-1, 128),
        "head_bias": head_bias.reshape(-1, 128),
        "seg_proj": seg_proj.T,
        "depth_proj": depth_proj.T,
        "normal_proj": normal_proj.T,
        "small_feats": small_feats,
        "small_labels": flat(small_labels),
        "small_depth": flat(small_depth),
        "small_normals": small_normals,
        "small_depth_valid": flat(small_depth_valid),
        "small_normal_valid": flat(small_normal_valid),
        "large_feats": large_feats,
        "large_labels": flat(large_labels),
        "large_depth": flat(large_depth),
        "large_normals": large_normals,
        "large_depth_valid": flat(large_depth_valid),
        "large_normal_valid": flat(large_normal_valid),
    }
    outputs = {
        "small_out_o": ((2 * WS, C), BF16),
        "large_out_o": ((2 * WL, C), BF16),
        "small_grad_o": ((2 * WS, WIDE), F32),
        "large_grad_o": ((2 * WL, WIDE), F32),
        "dk_o": ((TAPS, shape.unit, HEADS), BF16),
        "vec_o": ((2, 8, WIDE), F32),
        "head_vec_o": ((8, HEADS), F32),
        "proj_o": ((PROJ, HEADW), F32),
    }
    for index in range(3):
        if shape.inside:
            outputs[f"dw{index}_o"] = ((shape.rows[index], 2 * shape.wide[index]), BF16)
        else:
            outputs[f"dw{index}_o"] = ((shape.full[index], shape.wide[index]), BF16)
    scratch = scratch_of(shape)
    scratch["dscore"] = ((PROJ, LINE), F32)
    names = [*inputs, *outputs, *scratch, "send", "recv"]
    used = {}

    def call(room, *operands):
        return pl.pallas_call(
            functools.partial(fused, shape, names, used),
            out_shape=[jax.ShapeDtypeStruct(dims, kind) for dims, kind in outputs.values()],
            in_specs=[anywhere if name == "head_w" else vmem for name in inputs],
            out_specs=[vmem] * len(outputs),
            scratch_shapes=[pltpu.VMEM(dims, kind) for dims, kind in scratch.values()]
            + [pltpu.SemaphoreType.DMA((count,)) for count in room],
            compiler_params=pltpu.CompilerParams(
                collective_id=0, has_side_effects=True, vmem_limit_bytes=64 * 2**20 - 2**16
            ),
            name="fused",
        )(*operands)

    jax.eval_shape(functools.partial(call, (2048, 2048)), *inputs.values())
    got = dict(zip(outputs, call((used["send"], used["recv"]), *inputs.values())))
    if not shape.inside:
        for index in range(3):
            mine = lax.psum_scatter(got[f"dw{index}_o"].astype(F32), "dp", scatter_dimension=0, tiled=True)
            both = lax.all_gather(mine, "section", axis=0)
            got[f"dw{index}_o"] = both.transpose(1, 0, 2).reshape(shape.rows[index], -1)

    results = {
        "small_out": ((2 * WS, C), BF16),
        "large_out": ((2 * WL, C), BF16),
        "small_grad": ((2 * WS, WIDE), F32),
        "large_grad": ((2 * WL, WIDE), F32),
        "dw0": ((shape.rows[0], BOT), F32),
        "dw1": ((shape.rows[1], BOT), F32),
        "dw2": ((shape.rows[2], C), F32),
        "reduce_gain": ((1, BOT), F32),
        "reduce_bias": ((1, BOT), F32),
        "dilated_gain": ((1, BOT), F32),
        "dilated_bias": ((1, BOT), F32),
        "expand_gain": ((1, C), F32),
        "expand_bias": ((1, C), F32),
        "dk": ((TAPS * shape.unit, HEADS), F32),
        "head_gain": ((HEADS // 128, 128), F32),
        "head_bias": ((HEADS // 128, 128), F32),
        "seg_proj": ((NCLS, HEADW), F32),
        "depth_proj": ((1, HEADW), F32),
        "normal_proj": ((3, HEADW), F32),
    }
    final = pl.pallas_call(
        functools.partial(finish, [*got, *results]),
        out_shape=[jax.ShapeDtypeStruct(dims, kind) for dims, kind in results.values()],
        in_specs=[vmem] * len(got),
        out_specs=[vmem] * len(results),
        compiler_params=pltpu.CompilerParams(vmem_limit_bytes=64 * 2**20 - 2**16),
        name="finish",
    )(*got.values())
    vectors = ("gain", "bias")
    return tuple(
        value.reshape(-1) if name.endswith(vectors) else value.T if name.endswith("proj") else value
        for name, value in zip(results, final)
    )


def finish(names, *refs):
    env = dict(zip(names, refs))
    for name in ("small_out", "large_out", "small_grad", "large_grad"):
        env[name][...] = env[name + "_o"][...]
    for index in range(3):
        env[f"dw{index}"][...] = env[f"dw{index}_o"][...].astype(F32)
    taps, unit, _ = env["dk_o"].shape
    for tap in range(taps):
        env["dk"][tap * unit:(tap + 1) * unit, :] = env["dk_o"][tap].astype(F32)
    vec, head_vec = env["vec_o"], env["head_vec_o"]
    for section in range(2):
        for row, name in enumerate(("expand_gain", "expand_bias")):
            env[name][0:1, section * WIDE:(section + 1) * WIDE] = vec[section, row:row + 1, :]
        for part, name in enumerate(("dilated_gain", "dilated_bias", "reduce_gain", "reduce_bias")):
            env[name][0:1, section * HALF:(section + 1) * HALF] = vec[section, 2:3, part * HALF:(part + 1) * HALF]
    gain = head_vec[1:2, :] + head_vec[3:4, :]
    bias = head_vec[0:1, :] + head_vec[2:3, :]
    for part in range(HEADS // 128):
        cols = slice(part * 128, (part + 1) * 128)
        env["head_gain"][part:part + 1, :] = gain[:, cols]
        env["head_bias"][part:part + 1, :] = bias[:, cols]
    proj = env["proj_o"]
    env["seg_proj"][...] = proj[0:NCLS, :]
    env["depth_proj"][...] = proj[DEPTH_ROW:DEPTH_ROW + 1, :]
    env["normal_proj"][...] = proj[NORMAL_ROW:NORMAL_ROW + 3, :]


def solution(mesh):
    rows, vector = P("dp", None), P()
    pixels, parts = P("dp"), P(None, "dp")
    group = (rows, pixels, pixels, parts, pixels, pixels)
    in_specs = (rows, rows, rows) + (vector,) * 6 + (rows,) + (vector,) * 5 + group + group
    out_specs = (
        (rows, rows, P("dp", "section"), P("dp", "section"), rows, rows, rows)
        + (vector,) * 6
        + (rows,)
        + (vector,) * 5
    )
    return jax.shard_map(body, mesh=mesh, in_specs=in_specs, out_specs=out_specs, check_vma=False)
```

```python
import functools

import jax
import jax.numpy as jnp
from jax import lax
from jax.experimental import pallas as pl
from jax.experimental.pallas import tpu as pltpu
from jax.sharding import PartitionSpec as P

C = 2048
BOT = 512
HEADW = 256
NCLS = 13
WS = 48
WL = 80
HS = 36
HL = 60

EPS = 1e-05
RIDGE = 0.1
SWEEPS = 5

F32 = jnp.float32
BF16 = jnp.bfloat16
MESH = pl.DeviceIdType.MESH

LINE = WS + WL
SEGMENTS = ((0, WS), (WS, WL))
HEIGHTS = (HS, HL)
PIX = 2 * LINE
TEAM = 8
CH = C // TEAM
HALF = BOT // 2
WIDE = C // 2
HEADS = 3 * HEADW
TAPS = 9
PROJ = 32
DEPTH_ROW = 16
NORMAL_ROW = 24

NN = (((1,), (0,)), ((), ()))
NT = (((1,), (1,)), ((), ()))
TN = (((0,), (0,)), ((), ()))


def mm(left, right, dims=NN):
    return lax.dot_general(left, right, dims, preferred_element_type=F32)


def flip(rank, bits):
    out = rank
    for bit in (1, 2, 4):
        if bits & bit:
            out = out + bit * (1 - 2 * ((rank // bit) % 2))
    return out


def sigmoid(value):
    return 1.0 / (1.0 + jnp.exp(-value))


def silu(value):
    return value * sigmoid(value)


def slope(value):
    sigma = sigmoid(value)
    return sigma * (1.0 + value * (1.0 - sigma))


def seg_rows(lines):
    for line in range(lines):
        for group, (start, length) in enumerate(SEGMENTS):
            yield group, slice(line * LINE + start, line * LINE + start + length)


def position(rows):
    return lax.broadcasted_iota(jnp.int32, (rows, 1), 0) % LINE


def column_mask(rows, tap_col):
    place = position(rows)
    small = place < WS
    column = jnp.where(small, place, place - WS) + (2 * tap_col - 2)
    width = jnp.where(small, WS, WL)
    return ((column >= 0) & (column < width)).astype(F32)


def sideways(value, tap_col):
    rows = value.shape[0]
    if tap_col == 1:
        return value
    return pltpu.roll(value, (2 - 2 * tap_col) % rows, 0) * column_mask(rows, tap_col)


def jacobi_weights(gram):
    third = (gram[0, 0] + gram[1, 1] + gram[2, 2]) / 3.0 * RIDGE
    matrix = {(i, j): gram[min(i, j), max(i, j)] + (third if i == j else 0.0) for i in range(3) for j in range(3)}
    one, zero = jnp.ones_like(third), jnp.zeros_like(third)
    vectors = {(i, j): one if i == j else zero for i in range(3) for j in range(3)}
    for _ in range(SWEEPS):
        for p, q in ((0, 1), (0, 2), (1, 2)):
            up = 2.0 * matrix[p, q]
            across = matrix[q, q] - matrix[p, p]
            scale = jnp.maximum(jnp.abs(up), jnp.abs(across))
            still = scale == 0.0
            scale = jnp.where(still, 1.0, scale)
            up, across = up / scale, across / scale
            length = jnp.where(still, 1.0, jnp.sqrt(up * up + across * across))
            larger = jnp.sqrt(0.5 + 0.5 * jnp.abs(across) / length)
            smaller = 0.5 * up / (length * larger)
            sign = jnp.where(up < 0.0, -1.0, 1.0)
            cosine = jnp.where(still, 1.0, jnp.where(across >= 0.0, larger, jnp.abs(smaller)))
            sine = jnp.where(still, 0.0, jnp.where(across >= 0.0, smaller, sign * larger))
            for i in range(3):
                first, second = matrix[i, p], matrix[i, q]
                matrix[i, p] = first * cosine - second * sine
                matrix[i, q] = first * sine + second * cosine
                first, second = vectors[i, p], vectors[i, q]
                vectors[i, p] = first * cosine - second * sine
                vectors[i, q] = first * sine + second * cosine
            for j in range(3):
                first, second = matrix[p, j], matrix[q, j]
                matrix[p, j] = first * cosine - second * sine
                matrix[q, j] = first * sine + second * cosine
    values = [matrix[i, i] for i in range(3)]
    least = jnp.sqrt(jnp.minimum(jnp.minimum(values[0], values[1]), values[2]))
    alphas = []
    roots = [lax.rsqrt(value) for value in values]
    sums = [vectors[0, k] + vectors[1, k] + vectors[2, k] for k in range(3)]
    for t in range(3):
        alphas.append(least * sum(vectors[t, k] * roots[k] * sums[k] for k in range(3)))
    return alphas


class Links:
    def __init__(self, send, recv, partner):
        self.send, self.recv, self.partner = send, recv, partner
        self.used_send = self.used_recv = 0
        self.open = []

    def slots(self, count=1):
        first = self.used_recv
        self.used_recv += count
        assert self.used_recv <= self.recv.shape[0]
        return first

    def outs(self, count=1):
        first = self.used_send
        self.used_send += count
        assert self.used_send <= self.send.shape[0]
        return first

    def copy(self, src, dst, device, out, slot):
        return pltpu.make_async_remote_copy(
            src_ref=src, dst_ref=dst, send_sem=self.send.at[out], recv_sem=self.recv.at[slot],
            device_id=device, device_id_type=MESH,
        )

    def put(self, src, dst, device, slot, when=None):
        out = self.outs()
        if when is not None:
            device = tuple(jnp.where(when, to, near) for to, near in zip(device, self.partner))
        make = functools.partial(self.copy, src, dst, device, out, slot)
        if when is None:
            make().start()
            done = lambda: make().wait_send()
        else:
            pl.when(when)(lambda: make().start())
            done = lambda: pl.when(when)(lambda: make().wait_send())
        self.open.append(done)
        return done

    def put_or_keep(self, src, dst, device, slot, mine, when=True):
        pl.when(when & mine)(lambda: pltpu.make_async_copy(src, dst, self.recv.at[slot]).start())
        return self.put(src, dst, device, slot, when & jnp.logical_not(mine))

    def landed(self, dst, slot, when=None):
        wait = lambda: pltpu.make_async_copy(dst, dst, self.recv.at[slot]).wait()
        if when is None:
            wait()
        else:
            pl.when(when)(wait)

    def close(self):
        for done in self.open:
            done()
        self.open = []


def pieces(ref, start, count):
    rows = ref.shape[2]
    at = start
    while at < start + count:
        shard, first = at // rows, at % rows
        length = min(rows - first, start + count - at)
        yield (shard // 4, shard % 4, slice(first, first + length)), slice(at - start, at - start + length)
        at += length


def take_rows(ref, start, count):
    if len(ref.shape) == 2:
        return ref[start:start + count, :]
    found = [ref[(*place, slice(None))] for place, _ in pieces(ref, start, count)]
    return found[0] if len(found) == 1 else jnp.concatenate(found, axis=0)


def put_rows(ref, start, value):
    if len(ref.shape) == 2:
        ref[start:start + value.shape[0], :] = value
        return
    for place, rows in pieces(ref, start, value.shape[0]):
        ref[(*place, slice(None))] = value[rows, :]


def several(count, body):
    if count <= 4:
        for index in range(count):
            body(index)
    else:
        lax.fori_loop(0, count, lambda index, carry: (body(index), carry)[1], 0)


class Shapes:
    def __init__(self, dp):
        self.dp = dp
        self.planes = dp // 4
        self.teams = dp // TEAM
        self.unit = C // dp
        self.units_half = dp // (2 * TEAM)
        self.rows = (C // dp, TAPS * BOT // dp, BOT // dp)
        self.wide = (HALF, HALF, WIDE)
        self.full = (C, TAPS * BOT, BOT)
        self.inside = all(rows % 32 == 0 for rows in self.rows)
        self.borders = 2 * dp > min(HEIGHTS)


def scratch_of(shape):
    planes = shape.planes
    table = {
        "x": ((PIX, C), BF16),
        "xh": ((PIX, WIDE), BF16),
        "wback": ((planes // 2, 4, C // shape.dp, HALF) if shape.inside else (WIDE, HALF), BF16),
        "kernel": ((TAPS, 2, CH // 2, HEADS), BF16),
        "pre1": ((PIX, HALF), F32),
        "pre2": ((PIX, HALF), F32),
        "pre3": ((PIX, WIDE), F32),
        "act1": ((3, 2, PIX, HALF), BF16),
        "act1s": ((3, 3, 2, PIX, HALF), BF16),
        "patch2": ((PIX, TAPS * BOT), BF16),
        "act2": ((2, PIX, HALF), BF16),
        "outb": ((4, 2, PIX, CH // 2), BF16),
        "outs": ((3, 6, 2, PIX, CH // 2), BF16),
        "patch": ((PIX, TAPS * CH), BF16),
        "part": ((8, LINE, HEADS), BF16),
        "partm": ((8, 8, HEADS), F32),
        "parts": ((TEAM, LINE, HEADS), BF16),
        "partsm": ((TEAM, 8, HEADS), F32),
        "preh": ((LINE, HEADS), F32),
        "acth": ((LINE, HEADS), BF16),
        "dyh": ((LINE, HEADS), F32),
        "dph": ((LINE, HEADS), BF16),
        "dpx": ((6, 2, LINE, HEADS), BF16),
        "dps": ((3, 6, PIX, HEADW), BF16),
        "grads": ((3, 4, PIX, CH), F32),
        "doutb": ((4, PIX, CH), BF16),
        "dout": ((4, PIX, CH), BF16),
        "du": ((PIX, WIDE), F32),
        "dpre3": ((PIX, WIDE), BF16),
        "half2": ((2, PIX, HALF), F32),
        "half2r": ((PIX, HALF), F32),
        "dy2": ((PIX, HALF), F32),
        "dp2": ((3, PIX, HALF), BF16),
        "half1": ((2, PIX, HALF), F32),
        "half1r": ((PIX, HALF), F32),
        "dy1": ((PIX, HALF), F32),
        "dp1": ((2, PIX, HALF), BF16),
        "dks": ((TAPS, CH // 2, HEADS), BF16),
        "dkr": ((TAPS, CH // 2, HEADS), BF16),
        "dku": ((TAPS, CH // 2, HEADS), BF16),
        "dproj": ((PROJ, HEADW), F32),
        "head_norm": ((8, HEADS), F32),
        "tallies": ((4, LINE), F32),
        "marks": ((8, LINE), jnp.int32),
        "values": ((16, LINE), F32),
        "proj": ((PROJ, HEADS), BF16),
        "dkg": ((shape.teams, TAPS, shape.unit, HEADS), BF16),
    }
    for name, count, width in (
        ("s1", 4, HALF), ("s2", 4, HALF), ("s3", 4, WIDE), ("t3", 4, WIDE), ("t2", 4, HALF), ("t1", 4, HALF),
        ("sh", 8, HEADS), ("th", 8, HEADS),
    ):
        rows = 8 if name == "s1" else 4
        table[name + "a"] = ((count, rows, width), F32)
        table[name + "b"] = ((planes, rows, width), F32)
    for name, rows, width in (("gm", 8, 128), ("pj", PROJ, HEADW)):
        table[name + "a"] = ((8, rows, width), F32)
        table[name + "b"] = ((planes, rows, width), F32)
    for index in range(3):
        rows, wide = shape.rows[index], shape.wide[index]
        if shape.inside:
            table[f"w{index}"] = ((planes, 4, rows, wide), BF16)
            table[f"dw{index}"] = ((planes, 4, rows, wide), BF16)
            table[f"ra{index}"] = ((2, planes, 2, rows // 2, wide), BF16)
            table[f"rb{index}"] = ((2, planes, rows // 2, wide), BF16)
            table[f"rc{index}"] = ((planes, rows, wide), BF16)
    return table


def fused(shape, names, used, *refs):
    env = dict(zip(names, refs))
    r_ = lambda name: env[name]
    s = lax.axis_index("section")
    d = lax.axis_index("dp")
    dp, planes, teams = shape.dp, shape.planes, shape.teams
    other = 1 - s
    plane, spot = d // 4, d % 4
    team, rank = d // TEAM, d % TEAM
    partner = (other, d)
    links = Links(r_("send"), r_("recv"), partner)

    gate = pltpu.get_barrier_semaphore()
    total = 2 * dp
    me = s * dp + d

    def greet(offset, carry):
        to = (me + offset) % total
        pl.semaphore_signal(gate, inc=1, device_id=(to // dp, to % dp), device_id_type=MESH)
        return carry

    lax.fori_loop(1, total, greet, 0)

    x = r_("x")
    for line in range(2):
        x[line * LINE:line * LINE + WS, :] = r_("small_feats")[line * WS:(line + 1) * WS, :]
        x[line * LINE + WS:(line + 1) * LINE, :] = r_("large_feats")[line * WL:(line + 1) * WL, :]
    marks, values, proj = r_("marks"), r_("values"), r_("proj")
    head_norm = r_("head_norm")
    for row, name in enumerate(("head_gain", "head_bias")):
        for part in range(HEADS // 128):
            head_norm[row:row + 1, part * 128:(part + 1) * 128] = r_(name)[part:part + 1, :]

    def own_line(section):
        small, large = slice(section * WS, (section + 1) * WS), slice(section * WL, (section + 1) * WL)
        for row, name in enumerate(("labels", "depth_valid", "normal_valid")):
            marks[row:row + 1, 0:WS] = r_("small_" + name)[:, small]
            marks[row:row + 1, WS:LINE] = r_("large_" + name)[:, large]
        for row, count, name in ((0, 1, "depth"), (8, 3, "normals")):
            values[row:row + count, 0:WS] = r_("small_" + name)[:, small]
            values[row:row + count, WS:LINE] = r_("large_" + name)[:, large]

    for section in range(2):
        pl.when(s == section)(functools.partial(own_line, section))
    proj[...] = jnp.zeros(proj.shape, BF16)
    for task, (row, name) in enumerate(((0, "seg_proj"), (DEPTH_ROW, "depth_proj"), (NORMAL_ROW, "normal_proj"))):
        matrix = r_(name)[...]
        proj[row:row + matrix.shape[0], task * HEADW:(task + 1) * HEADW] = matrix
    xh = r_("xh")
    xh_slot = links.slots()
    pltpu.make_async_copy(x.at[:, pl.ds(pl.multiple_of(s * WIDE, WIDE), WIDE)], xh, links.recv.at[xh_slot]).start()
    pl.semaphore_wait(gate, total - 1)

    def plane_sum(key, width_of):
        near = r_(key + "a")
        count = near.shape[0]
        own = spot if count == 4 else 4 * s + spot
        first = links.slots(count)
        for bits in range(1, count):
            to = flip(own, bits)
            device = (s, 4 * plane + to) if count == 4 else (to // 4, 4 * plane + to % 4)
            links.put(near.at[own], near.at[own], device, first + bits)

        def finish():
            for bits in range(1, count):
                links.landed(near.at[flip(own, bits)], first + bits)
            acc = near[0]
            for index in range(1, count):
                acc = acc + near[index]
            return acc

        return finish

    def line_sum(key, value):
        far = r_(key + "b")
        far[plane] = value
        first, out = links.slots(planes), links.outs(planes)

        def make(offset):
            to = (plane + offset) % planes
            return links.copy(far.at[plane], far.at[plane], (s, 4 * to + spot), out + offset, first + offset)

        several(planes - 1, lambda i: make(i + 1).start())
        links.open.append(lambda: several(planes - 1, lambda i: make(i + 1).wait_send()))

        def finish():
            several(planes - 1, lambda i: links.landed(far.at[0], first + i + 1))
            acc = far[0]
            for index in range(1, planes):
                acc = acc + far[index]
            return acc

        return finish

    def add_up(key):
        return line_sum(key, plane_sum(key, None)())()

    def own_slot(key):
        near = r_(key + "a")
        return near.at[spot if near.shape[0] == 4 else 4 * s + spot]

    def put_stats(key, rows, first, second=None):
        slot = own_slot(key)
        for group in range(2):
            a = b = None
            for g, rng in seg_rows(rows):
                if g == group:
                    one, two = first(g, rng), second(g, rng)
                    one, two = jnp.sum(one, axis=0, keepdims=True), jnp.sum(two, axis=0, keepdims=True)
                    a, b = (one, two) if a is None else (a + one, b + two)
            slot[2 * group:2 * group + 1, :] = a
            slot[2 * group + 1:2 * group + 2, :] = b

    counts = (2.0 * dp * WS, 2.0 * dp * WL)

    def moments(sums):
        means, invs = [], []
        for group in range(2):
            mean = sums[2 * group:2 * group + 1, :] / counts[group]
            var = sums[2 * group + 1:2 * group + 2, :] / counts[group] - mean * mean
            means.append(mean)
            invs.append(lax.rsqrt(var + EPS))
        return means, invs

    gathers = []
    if shape.inside:
        shards = (
            r_("reduce_w").at[:, pl.ds(pl.multiple_of(s * HALF, HALF), HALF)],
            r_("dilated_w").at[:, pl.ds(pl.multiple_of(s * HALF, HALF), HALF)],
            r_("expand_w").at[:, pl.ds(pl.multiple_of(s * WIDE, WIDE), WIDE)],
        )
        near_x, near_y, corner = flip(spot, 1), flip(spot, 2), flip(spot, 3)
        at_x, at_y = (s, 4 * plane + near_x), (s, 4 * plane + near_y)

        def gather(index):
            rows, wide = shape.rows[index], shape.wide[index]
            buf = r_(f"w{index}")
            cut = rows // 2
            first, out = links.slots(planes), links.outs(planes)
            mine = pltpu.make_async_copy(shards[index], buf.at[plane, spot], links.recv.at[first])
            mine.start()

            def make(offset):
                to = (plane + offset) % planes
                return links.copy(shards[index], buf.at[plane, spot], (s, 4 * to + spot), out + offset, first + offset)

            several(planes - 1, lambda i: make(i + 1).start())
            links.open.append(lambda: several(planes - 1, lambda i: make(i + 1).wait_send()))
            up, low = pl.ds(0, cut), pl.ds(cut, cut)
            slot = links.slots(6)
            yield
            mine.wait()
            several(planes - 1, lambda i: links.landed(buf.at[0, 0], first + i + 1))
            links.put(buf.at[:, spot, up], buf.at[:, spot, up], at_x, slot)
            links.put(buf.at[:, spot, low], buf.at[:, spot, low], at_y, slot + 1)
            links.put(buf.at[:, spot, up], buf.at[:, spot, up], at_y, slot + 2)
            links.put(buf.at[:, spot, low], buf.at[:, spot, low], at_x, slot + 3)
            yield
            links.landed(buf.at[:, near_x, up], slot)
            links.put(buf.at[:, near_x, up], buf.at[:, near_x, up], at_y, slot + 4)
            links.landed(buf.at[:, near_y, low], slot + 1)
            links.put(buf.at[:, near_y, low], buf.at[:, near_y, low], at_x, slot + 5)
            yield
            links.landed(buf.at[:, near_y, up], slot + 2)
            links.landed(buf.at[:, near_x, low], slot + 3)
            links.landed(buf.at[:, corner, up], slot + 4)
            links.landed(buf.at[:, corner, low], slot + 5)
            yield

        gathers = [gather(index) for index in range(3)]
        for one in gathers:
            next(one)
        weights = [r_(f"w{index}") for index in range(3)]
    else:
        weights = [r_("reduce_w"), r_("dilated_w"), r_("expand_w")]

    def gather_on(index):
        if shape.inside:
            next(gathers[index])

    kernel = r_("kernel")
    unit, halves = shape.unit, shape.units_half
    share = 2 * halves
    kernel_slot = links.slots(TAPS * halves)
    kernel_out = links.outs(TAPS * teams)

    def unit_at(index):
        number = TAPS * d + index
        tap, chunk = number // dp, number % dp
        inner = chunk % share
        return inner // halves == s, chunk // share, tap, inner % halves

    def kernel_copy(index, to_team):
        sends, to_rank, tap, place = unit_at(index)
        src = r_("head_w").at[index]
        dst = kernel.at[tap, s, pl.ds(pl.multiple_of(place * unit, unit), unit)]
        to = to_team * TEAM + to_rank
        slot = kernel_slot + tap * halves + place
        to_core = jnp.where(to == d, other, s)
        remote = lambda: links.copy(src, dst, (to_core, to), kernel_out + index * teams + to_team, slot)
        local = lambda: pltpu.make_async_copy(src, dst, links.recv.at[slot])
        return sends, to == d, remote, local

    def kernel_start(index, to_team):
        sends, mine, remote, local = kernel_copy(index, to_team)
        pl.when(sends & mine)(lambda: local().start())
        pl.when(sends & jnp.logical_not(mine))(lambda: remote().start())

    def kernel_done(index, to_team):
        sends, mine, remote, _ = kernel_copy(index, to_team)
        pl.when(sends & jnp.logical_not(mine))(lambda: remote().wait_send())

    def kernel_send():
        lax.fori_loop(0, TAPS * teams, lambda i, c: (kernel_start(i // teams, i % teams), c)[1], 0)

    links.open.append(lambda: lax.fori_loop(0, TAPS * teams, lambda i, c: (kernel_done(i // teams, i % teams), c)[1], 0))

    def same_image(block, tap_row):
        near = block + (tap_row - 1)
        inside = (near >= 0) & (near < dp)
        return [inside & ((2 * near + 2 * height) // height == (2 * block + 2 * height) // height) for height in HEIGHTS]

    def row_mask(block, tap_row, rows=PIX):
        small, large = [flag.astype(F32) for flag in same_image(block, tap_row)]
        return jnp.where(position(rows) < WS, small, large)

    def own_part(name, width):
        return r_(name)[0:1, pl.ds(pl.multiple_of(s * width, width), width)]

    norm1 = own_part("reduce_gain", HALF), own_part("reduce_bias", HALF)
    norm2 = own_part("dilated_gain", HALF), own_part("dilated_bias", HALF)
    norm3 = own_part("expand_gain", WIDE), own_part("expand_bias", WIDE)
    pre1, pre2, pre3 = r_("pre1"), r_("pre2"), r_("pre3")
    act1, act2 = r_("act1"), r_("act2")
    squares = lambda ref: (lambda g, rng: ref[rng, :], lambda g, rng: ref[rng, :] * ref[rng, :])

    gather_on(0)
    gather_on(0)
    gather_on(1)
    kernel_send()
    gather_on(0)
    pre1[...] = mm(x[...], take_rows(weights[0], 0, C))
    back_slot = links.slots()
    half_planes = planes // 2

    def rows_half(section):
        if shape.inside:
            return weights[0].at[pl.ds(pl.multiple_of(section * half_planes, half_planes), half_planes)]
        return weights[0].at[pl.ds(pl.multiple_of(section * WIDE, WIDE), WIDE)]

    links.put(rows_half(other), r_("wback"), partner, back_slot)
    put_stats("s1", 2, *squares(pre1))
    slot_ref = own_slot("s1")
    slot_ref[4:8, :] = jnp.zeros((4, HALF), F32)
    lane = lax.broadcasted_iota(jnp.int32, (1, LINE), 1)
    tally = jnp.zeros((1, LINE), F32)
    for number, name in enumerate(("labels", "depth_valid", "normal_valid")):
        for group, size in enumerate(("small_", "large_")):
            value = r_(size + name)[...]
            keep = (value >= 0).astype(F32) if number == 0 else value.astype(F32)
            count = jnp.sum(keep, axis=1, keepdims=True)
            tally = tally + jnp.where(lane == 2 * number + group, count, 0.0)
    slot_ref[4:5, 0:LINE] = tally
    gather_on(1)
    gather_on(2)
    sums = add_up("s1")
    mean1, inv1 = moments(sums)
    tallies = r_("tallies")
    tallies[...] = sums[4:8, 0:LINE]
    gain, bias = norm1
    for group, rng in seg_rows(2):
        hat = (pre1[rng, :] - mean1[group]) * inv1[group]
        pre1[rng, :] = hat
        act1[1, s, rng, :] = silu(hat * gain + bias).astype(BF16)
    slot = links.slots(5)
    above, below = jnp.maximum(d - 1, 0), jnp.minimum(d + 1, dp - 1)
    has_above, has_below = d > 0, d < dp - 1
    links.put(act1.at[1, s], act1.at[2, s], (s, above), slot + 1 + s, has_above)
    links.put(act1.at[1, s], act1.at[0, s], (s, below), slot + 3 + s, has_below)
    links.put(act1.at[1, s], act1.at[1, s], partner, slot)

    @pl.when(jnp.logical_not(has_above))
    def _():
        act1[0] = jnp.zeros(act1.shape[1:], BF16)

    @pl.when(jnp.logical_not(has_below))
    def _():
        act1[2] = jnp.zeros(act1.shape[1:], BF16)

    act1s, patch2 = r_("act1s"), r_("patch2")
    gather_on(2)

    def spread_rows(tap_row, half):
        value = act1[tap_row, half].astype(F32)
        if tap_row != 1 and shape.borders:
            value = value * row_mask(d, tap_row)
        for tap_col in range(3):
            piece = sideways(value, tap_col).astype(BF16)
            at = (3 * tap_row + tap_col) * BOT + half * HALF
            act1s[tap_col, tap_row, half] = piece
            patch2[:, at:at + HALF] = piece

    links.landed(act1.at[1, other], slot)
    for half in range(2):
        spread_rows(1, half)
    links.landed(act1.at[2, s], slot + 1 + s, has_below)
    links.put(act1.at[2, s], act1.at[2, s], partner, slot + 1 + s, has_below)
    links.landed(act1.at[0, s], slot + 3 + s, has_above)
    links.put(act1.at[0, s], act1.at[0, s], partner, slot + 3 + s, has_above)
    links.landed(act1.at[2, other], slot + 1 + other, has_below)
    for half in range(2):
        spread_rows(2, half)
    links.landed(act1.at[0, other], slot + 3 + other, has_above)
    for half in range(2):
        spread_rows(0, half)
    gather_on(1)
    pre2[...] = mm(patch2[...], take_rows(weights[1], 0, TAPS * BOT))
    put_stats("s2", 2, *squares(pre2))
    mean2, inv2 = moments(add_up("s2"))
    gain, bias = norm2
    for group, rng in seg_rows(2):
        hat = (pre2[rng, :] - mean2[group]) * inv2[group]
        pre2[rng, :] = hat
        act2[s, rng, :] = silu(hat * gain + bias).astype(BF16)
    slot = links.slots()
    links.put(act2.at[s], act2.at[s], partner, slot)
    gather_on(2)
    links.landed(act2.at[other], slot)
    pre3[...] = mm(act2[0], take_rows(weights[2], 0, HALF)) + mm(act2[1], take_rows(weights[2], HALF, HALF))
    put_stats("s3", 2, *squares(pre3))
    mean3, inv3 = moments(add_up("s3"))
    links.landed(xh, xh_slot)
    gain, bias = norm3
    outb = r_("outb")
    for group, rng in seg_rows(2):
        hat = (pre3[rng, :] - mean3[group]) * inv3[group]
        pre3[rng, :] = hat
        value = silu(hat * gain + bias + xh[rng, :].astype(F32)).astype(BF16)
        for part in range(4):
            for half in range(2):
                at = part * CH + half * (CH // 2)
                outb[part, half, rng, :] = value[:, at:at + CH // 2]
        start, length = SEGMENTS[group]
        line = rng.start // LINE
        whole = r_(("small_out_o", "large_out_o")[group])
        whole[line * length:(line + 1) * length, pl.ds(pl.multiple_of(s * WIDE, WIDE), WIDE)] = value

    outs = r_("outs")
    seat = rank // 4
    slot = links.slots(6)
    for part in range(4):
        to_rank = 4 * s + part
        src = outb.at[part]
        chip = team * TEAM + to_rank
        links.put_or_keep(src, outs.at[1, rank % 4 + 1], (seat, chip), slot + rank % 4 + 1, (seat == s) & (part == rank % 4))
    out_slot = links.slots(2)
    out_parts = [r_(name).at[:, pl.ds(pl.multiple_of(s * WIDE, WIDE), WIDE)] for name in ("small_out_o", "large_out_o")]
    for index, out_part in enumerate(out_parts):
        links.put(out_part, out_part, partner, out_slot + index)
    has_low = (s == 1) | (team > 0)
    has_high = (s == 0) | (team < teams - 1)

    @pl.when(jnp.logical_not(has_low))
    def _():
        outs[1, 0] = jnp.zeros((2, PIX, CH // 2), BF16)

    @pl.when(jnp.logical_not(has_high))
    def _():
        outs[1, 5] = jnp.zeros((2, PIX, CH // 2), BF16)

    near_block, near_border = 4 - 3 * s, 5 * s
    far_block, far_border = 1 + 3 * s, 5 - 5 * s
    far_chip = (other, jnp.clip(d + TEAM * (2 * s - 1), 0, dp - 1))
    has_far = (has_low & (s == 0)) | (has_high & (s == 1))
    for index in range(1, 5):
        links.landed(outs.at[1, index], slot + index)
    links.put(outs.at[1, near_block], outs.at[1, near_border], partner, slot + near_border)
    links.put(outs.at[1, far_block], outs.at[1, far_border], far_chip, slot + far_border, has_far)

    swap_slot = links.slots()
    several(TAPS * halves, lambda i: links.landed(kernel.at[0, 0, pl.ds(0, unit)], kernel_slot + i))
    links.put(kernel.at[:, s], kernel.at[:, s], partner, swap_slot)

    def widen(index, carry):
        for half in range(2):
            value = outs[1, index, half].astype(F32)
            outs[0, index, half] = sideways(value, 0).astype(BF16)
            outs[2, index, half] = sideways(value, 2).astype(BF16)
        return carry

    lax.fori_loop(1, 5, widen, 0)
    links.landed(kernel.at[:, other], swap_slot)

    first_block = team * TEAM + 4 * s
    patch, part, partm = r_("patch"), r_("part"), r_("partm")
    parts, partsm = r_("parts"), r_("partsm")
    part_slot = links.slots(2 * TEAM)

    def head_block(index):
        for tap_row in range(3):
            for tap_col in range(3):
                for half in range(2):
                    piece = outs[tap_col, index + tap_row, half]
                    if tap_row != 1 and shape.borders:
                        piece = piece * row_mask(first_block + index, tap_row).astype(BF16)
                    at = (3 * tap_row + tap_col) * CH + half * (CH // 2)
                    patch[:, at:at + CH // 2] = piece
        value = mm(patch[...], kernel[...].reshape(TAPS * CH, HEADS))
        for line in range(2):
            number = 2 * index + line
            for group, (start, length) in enumerate(SEGMENTS):
                rows = value[line * LINE + start:line * LINE + start + length, :]
                middle = jnp.mean(rows, axis=0, keepdims=True)
                partm[number, group:group + 1, :] = middle
                part[number, start:start + length, :] = (rows - middle).astype(BF16)
            chip = team * TEAM + 4 * s + index
            mine = (4 * s + index == rank) & (s == line)
            links.put_or_keep(part.at[number], parts.at[rank], (line, chip), part_slot + rank, mine)
            links.put_or_keep(partm.at[number], partsm.at[rank], (line, chip), part_slot + TEAM + rank, mine)

    head_block(1)
    head_block(2)
    links.landed(outs.at[1, 0], slot, has_low)
    links.landed(outs.at[1, 5], slot + 5, has_high)
    widen(0, 0)
    widen(5, 0)
    head_block(0)
    head_block(3)

    for index in range(TEAM):
        links.landed(parts.at[index], part_slot + index)
        links.landed(partsm.at[index], part_slot + TEAM + index)
    preh, acth, dyh = r_("preh"), r_("acth"), r_("dyh")
    for group, (start, length) in enumerate(SEGMENTS):
        rng = slice(start, start + length)
        acc = sum(parts[index, rng, :].astype(F32) for index in range(TEAM))
        acc = acc + sum(partsm[index, group:group + 1, :] for index in range(TEAM))
        preh[rng, :] = acc

    labels, depth, normals = marks[0:1, :], values[0:1, :], values[8:11, :]
    seg_keep = (labels >= 0).astype(F32)
    depth_keep, normal_keep = marks[1:2, :].astype(F32), marks[2:3, :].astype(F32)
    small_lane = lane < WS
    put_stats("sh", 1, *squares(preh))
    sums = add_up("sh")
    meanh, invh = moments(sums)
    tally = tallies[0:1, :]

    def pixel_count(number):
        picked = [jnp.sum(jnp.where(lane == 2 * number + group, tally, 0.0), axis=1, keepdims=True) for group in range(2)]
        return jnp.maximum(jnp.where(small_lane, picked[0], picked[1]), 1.0)

    gain, bias = head_norm[0:1, :], head_norm[1:2, :]
    for group, rng in seg_rows(1):
        hat = (preh[rng, :] - meanh[group]) * invh[group]
        preh[rng, :] = hat
        acth[rng, :] = silu(hat * gain + bias).astype(BF16)

    scores = mm(proj[...], acth[...], NT)
    row = lax.broadcasted_iota(jnp.int32, (16, LINE), 0)
    logits = jnp.where(row < NCLS, scores[0:16, :], -1e30)
    top = jnp.max(logits, axis=0, keepdims=True)
    power = jnp.where(row < NCLS, jnp.exp(logits - top), 0.0)
    soft = power / jnp.sum(power, axis=0, keepdims=True)
    onehot = (row == labels).astype(F32)
    d_logits = (soft - onehot) * (seg_keep / pixel_count(0))
    gap = scores[DEPTH_ROW:DEPTH_ROW + 1, :] - depth
    d_depth = depth_keep / pixel_count(1) * gap * lax.rsqrt(gap * gap + 1.0)
    guess = scores[NORMAL_ROW:NORMAL_ROW + 3, :]
    inverse = lax.rsqrt(jnp.sum(guess * guess, axis=0, keepdims=True) + 1.0)
    along = jnp.sum(guess * normals, axis=0, keepdims=True)
    weight = normal_keep / pixel_count(2)
    d_guess = r_("dscore")
    d_guess[...] = jnp.zeros(d_guess.shape, F32)
    d_guess[0:16, :] = d_logits
    d_guess[DEPTH_ROW:DEPTH_ROW + 1, :] = d_depth
    d_guess[NORMAL_ROW:NORMAL_ROW + 3, :] = -weight * (normals * inverse - along * (inverse * inverse * inverse) * guess)
    d_scores = d_guess[...]
    high = d_scores.astype(BF16)
    low = (d_scores - high.astype(F32)).astype(BF16)
    d_act = mm(high, proj[...], TN) + mm(low, proj[...], TN)
    value = mm(high, acth[...]) + mm(low, acth[...])
    d_proj = r_("dproj")
    d_proj[0:16, :] = value[0:16, 0:HEADW]
    d_proj[16:24, :] = value[16:24, HEADW:2 * HEADW]
    d_proj[24:32, :] = value[24:32, 2 * HEADW:]
    for group, rng in seg_rows(1):
        dyh[rng, :] = d_act[rng, :] * slope(preh[rng, :] * gain + bias)
    put_stats("th", 1, lambda g, rng: dyh[rng, :], lambda g, rng: dyh[rng, :] * preh[rng, :])
    sums = add_up("th")
    r_("head_vec_o")[...] = sums
    dph, dpx = r_("dph"), r_("dpx")
    for group, rng in seg_rows(1):
        first, second = sums[2 * group:2 * group + 1, :], sums[2 * group + 1:2 * group + 2, :]
        value = dyh[rng, :] - first / counts[group] - preh[rng, :] * (second / counts[group])
        dph[rng, :] = (gain * invh[group] * value).astype(BF16)

    slot = links.slots(12)
    place = rank % 4 + 1
    for step in range(TEAM):
        chip = team * TEAM + flip(rank, step)
        if step == 0:
            links.put_or_keep(dph, dpx.at[place, s], (seat, chip), slot + 2 * place + s, seat == s)
        else:
            links.put(dph, dpx.at[place, s], (seat, chip), slot + 2 * place + s)

    @pl.when(jnp.logical_not(has_low))
    def _():
        dpx[0] = jnp.zeros((2, LINE, HEADS), BF16)

    @pl.when(jnp.logical_not(has_high))
    def _():
        dpx[5] = jnp.zeros((2, LINE, HEADS), BF16)

    for index in range(2, 10):
        links.landed(dpx.at[index // 2, index % 2], slot + index)
    links.put(dpx.at[near_block], dpx.at[near_border], partner, slot + 2 * near_border)
    links.put(dpx.at[far_block], dpx.at[far_border], far_chip, slot + 2 * far_border, has_far)
    border_slot = slot

    dks, dkr, dku, dkg = r_("dks"), r_("dkr"), r_("dku"), r_("dkg")

    def tap_grad(tap, half):
        tap_row, tap_col = tap // 3, tap % 3
        acc = None
        for index in range(4):
            left = outs[tap_col, index + tap_row, half]
            right = dpx[index + 1].reshape(PIX, HEADS)
            if shape.borders:
                right = right * row_mask(first_block + index, tap_row).astype(BF16)
            term = mm(left, right, TN)
            acc = term if acc is None else acc + term
        return acc

    def their_tap(tap, carry):
        dks[tap] = tap_grad(tap, other).astype(BF16)
        return carry

    lax.fori_loop(0, TAPS, their_tap, 0)
    swap_slot = links.slots()
    links.put(dks, dkr, partner, swap_slot)
    def my_tap(tap, carry):
        dku[tap] = tap_grad(tap, s).astype(BF16)
        return carry

    lax.fori_loop(0, TAPS, my_tap, 0)
    links.landed(dkr, swap_slot)

    def both(tap, carry):
        dku[tap] = (dku[tap].astype(F32) + dkr[tap].astype(F32)).astype(BF16)
        return carry

    lax.fori_loop(0, TAPS, both, 0)

    grad_slot = links.slots(teams * TAPS)
    grad_out = links.outs(TAPS * halves)

    def grad_copy(number):
        tap, place = number // halves, number % halves
        chunk = rank * share + s * halves + place
        overall = tap * dp + chunk
        owner, index = overall // TAPS, overall % TAPS
        src = dku.at[tap, pl.ds(pl.multiple_of(place * unit, unit), unit)]
        dst = dkg.at[team, index]
        at = grad_slot + team * TAPS + index
        to_core = jnp.where(owner == d, other, s)
        remote = lambda: links.copy(src, dst, (to_core, owner), grad_out + number, at)
        local = lambda: pltpu.make_async_copy(src, dst, links.recv.at[at])
        return owner == d, remote, local

    def grad_start(number):
        mine, remote, local = grad_copy(number)
        pl.when(mine)(lambda: local().start())
        pl.when(jnp.logical_not(mine))(lambda: remote().start())

    def grad_done(number):
        mine, remote, _ = grad_copy(number)
        pl.when(jnp.logical_not(mine))(lambda: remote().wait_send())

    lax.fori_loop(0, TAPS * halves, lambda i, c: (grad_start(i), c)[1], 0)
    links.open.append(lambda: lax.fori_loop(0, TAPS * halves, lambda i, c: (grad_done(i), c)[1], 0))
    links.landed(dpx.at[0], border_slot, has_low)
    links.landed(dpx.at[5], border_slot + 10, has_high)

    dps, grads = r_("dps"), r_("grads")
    for task in range(3):
        cols = slice(task * HEADW, (task + 1) * HEADW)

        def spread(index, carry):
            piece = dpx[index, :, :, cols].reshape(PIX, HEADW)
            value = piece.astype(F32)
            dps[1, index] = piece
            dps[0, index] = sideways(value, 0).astype(BF16)
            dps[2, index] = sideways(value, 2).astype(BF16)
            return carry

        lax.fori_loop(0, 6, spread, 0)

        def pull(index, carry):
            acc = None
            for tap_row in range(3):
                for tap_col in range(3):
                    piece = dps[tap_col, index + tap_row]
                    if tap_row != 1 and shape.borders:
                        piece = piece * row_mask(first_block + index, tap_row).astype(BF16)
                    tap = 8 - (3 * tap_row + tap_col)
                    term = mm(piece, kernel[tap, :, :, cols].reshape(CH, HEADW), NT)
                    acc = term if acc is None else acc + term
            grads[task, index] = acc
            return carry

        lax.fori_loop(0, 4, pull, 0)

    pairs = [(i, j) for i in range(3) for j in range(i, 3)]

    def dots(index, sums):
        sums = list(sums)
        for group, rng in seg_rows(2):
            block = [grads[task, index, rng, :] for task in range(3)]
            for number, (i, j) in enumerate(pairs):
                sums[len(pairs) * group + number] += jnp.sum(block[i] * block[j], axis=0, keepdims=True)
        return tuple(sums)

    sums = lax.fori_loop(0, 4, dots, (jnp.zeros((1, CH), F32),) * (2 * len(pairs)))
    tally = jnp.zeros((8, LINE), F32)
    for number, total_row in enumerate(sums):
        tally = tally + jnp.where(lane == number, jnp.sum(total_row, axis=1, keepdims=True), 0.0)
    own_slot("gm")[...] = tally
    near_done = plane_sum("gm", None)


    far_done = line_sum("gm", near_done())
    gram_row = far_done()[0:1, :]
    dot_of = [jnp.sum(jnp.where(lane == k, gram_row, 0.0), axis=1, keepdims=True) for k in range(2 * len(pairs))]
    gram = {
        pair: jnp.where(lane == 0, dot_of[k], dot_of[len(pairs) + k]) for k, pair in enumerate(pairs)
    }
    alphas = jacobi_weights(gram)
    alphas = [[alpha[:, group:group + 1] for alpha in alphas] for group in range(2)]

    doutb, dout = r_("doutb"), r_("dout")
    slot = links.slots(4)
    for index in range(4):
        for group, rng in seg_rows(2):
            aligned = sum(alphas[group][task] * grads[task, index, rng, :] for task in range(3))
            doutb[index, rng, :] = aligned.astype(BF16)
        chip = team * TEAM + 4 * s + index
        links.put_or_keep(
            doutb.at[index], dout.at[rank % 4], (seat, chip), slot + rank % 4, (seat == s) & (rank % 4 == index)
        )

    own_slot("pj")[...] = d_proj[...]
    proj_near = plane_sum("pj", None)

    for index in range(4):
        links.landed(dout.at[index], slot + index)
    du, dpre3 = r_("du"), r_("dpre3")
    gain, bias = norm3
    for group, rng in seg_rows(2):
        at = slope(pre3[rng, :] * gain + bias + xh[rng, :].astype(F32))
        for part_index in range(4):
            cols = slice(part_index * CH, (part_index + 1) * CH)
            du[rng, cols] = dout[part_index, rng, :].astype(F32) * at[:, cols]
    vec = r_("vec_o")
    with_hat = lambda dy, hat: (lambda g, rng: dy[rng, :], lambda g, rng: dy[rng, :] * hat[rng, :])
    put_stats("t3", 2, *with_hat(du, pre3))
    sums = add_up("t3")
    vec[s, 0:1, :] = sums[1:2, :] + sums[3:4, :]
    vec[s, 1:2, :] = sums[0:1, :] + sums[2:3, :]

    def norm_back(sums, group, rng, dy, hat, scale):
        first, second = sums[2 * group:2 * group + 1, :], sums[2 * group + 1:2 * group + 2, :]
        return scale * (dy[rng, :] - first / counts[group] - hat[rng, :] * (second / counts[group]))

    for group, rng in seg_rows(2):
        dpre3[rng, :] = norm_back(sums, group, rng, du, pre3, gain * inv3[group]).astype(BF16)
    half2, half2r = r_("half2"), r_("half2r")
    value = mm(dpre3[...], take_rows(weights[2], 0, BOT), NT)
    half2[0], half2[1] = value[:, :HALF], value[:, HALF:]
    slot = links.slots()
    links.put(half2.at[other], half2r, partner, slot)

    def scatter(index):
        rows, wide = shape.rows[index], shape.wide[index]
        cut = rows // 2
        up, low = pl.ds(0, cut), pl.ds(cut, cut)
        buf = r_(f"dw{index}")
        ra, rb, rc = r_(f"ra{index}"), r_(f"rb{index}"), r_(f"rc{index}")
        slot = links.slots(6)
        links.put(buf.at[:, near_y, up], ra.at[0, :, 0], at_y, slot)
        links.put(buf.at[:, corner, up], ra.at[0, :, 1], at_y, slot + 1)
        links.put(buf.at[:, near_x, low], ra.at[1, :, 0], at_x, slot + 2)
        links.put(buf.at[:, corner, low], ra.at[1, :, 1], at_x, slot + 3)
        yield

        def add(at, part, extra):
            total = buf[:, at, part].astype(F32) + extra.astype(F32)
            buf[:, at, part] = total.astype(BF16)

        links.landed(ra.at[0, :, 1], slot + 1)
        add(near_x, up, ra[0, :, 1])
        links.put(buf.at[:, near_x, up], rb.at[0], at_x, slot + 4)
        links.landed(ra.at[1, :, 1], slot + 3)
        add(near_y, low, ra[1, :, 1])
        links.put(buf.at[:, near_y, low], rb.at[1], at_y, slot + 5)
        yield
        links.landed(ra.at[0, :, 0], slot)
        links.landed(ra.at[1, :, 0], slot + 2)
        links.landed(rb.at[0], slot + 4)
        add(spot, up, ra[0, :, 0].astype(F32) + rb[0].astype(F32))
        links.landed(rb.at[1], slot + 5)
        add(spot, low, ra[1, :, 0].astype(F32) + rb[1].astype(F32))
        first, out = links.slots(planes), links.outs(planes)

        def make(offset):
            to = (plane + offset) % planes
            return links.copy(buf.at[to, spot], rc.at[plane], (s, 4 * to + spot), out + offset, first + offset)

        several(planes - 1, lambda i: make(i + 1).start())
        links.open.append(lambda: several(planes - 1, lambda i: make(i + 1).wait_send()))
        rc[plane] = buf[plane, spot]
        yield
        several(planes - 1, lambda i: links.landed(rc.at[0], first + i + 1))
        acc = rc[0].astype(F32)
        for number in range(1, planes):
            acc = acc + rc[number].astype(F32)
        result = r_(f"dw{index}_o")
        mine = pl.ds(pl.multiple_of(s * wide, wide), wide)
        result[:, mine] = acc.astype(BF16)
        at = links.slots()
        links.put(result.at[:, mine], result.at[:, mine], partner, at)
        yield
        links.landed(result.at[:, mine], at)
        yield

    def advance(one):
        if one is not None:
            next(one)

    def reduced(index):
        if not shape.inside:
            return None
        one = scatter(index)
        next(one)
        return one

    grad_of = lambda index: r_(f"dw{index}") if shape.inside else r_(f"dw{index}_o")
    for half in range(2):
        put_rows(grad_of(2), half * HALF, mm(act2[half], dpre3[...], TN).astype(BF16))
    third = reduced(2)

    links.landed(half2r, slot)
    dy2, dp2 = r_("dy2"), r_("dp2")
    gain, bias = norm2
    for group, rng in seg_rows(2):
        value = half2[s, rng, :] + half2r[rng, :]
        dy2[rng, :] = value * slope(pre2[rng, :] * gain + bias)
    put_stats("t2", 2, *with_hat(dy2, pre2))
    sums = add_up("t2")
    vec[s, 2:3, 0:HALF] = sums[1:2, :] + sums[3:4, :]
    vec[s, 2:3, HALF:2 * HALF] = sums[0:1, :] + sums[2:3, :]
    for group, rng in seg_rows(2):
        dp2[1, rng, :] = norm_back(sums, group, rng, dy2, pre2, gain * inv2[group]).astype(BF16)
    slot = links.slots(2)
    links.put(dp2.at[1], dp2.at[2], (s, above), slot, has_above)
    links.put(dp2.at[1], dp2.at[0], (s, below), slot + 1, has_below)
    advance(third)

    @pl.when(jnp.logical_not(has_above))
    def _():
        dp2[0] = jnp.zeros((PIX, HALF), BF16)

    @pl.when(jnp.logical_not(has_below))
    def _():
        dp2[2] = jnp.zeros((PIX, HALF), BF16)

    for tap in range(TAPS):
        for half in range(2):
            at = tap * BOT + half * HALF
            put_rows(grad_of(1), at, mm(act1s[tap % 3, tap // 3, half], dp2[1], TN).astype(BF16))
    second = reduced(1)
    links.landed(dp2.at[2], slot, has_below)
    links.landed(dp2.at[0], slot + 1, has_above)
    acc = None
    for tap_row in range(3):
        value = dp2[tap_row].astype(F32)
        if tap_row != 1 and shape.borders:
            value = value * row_mask(d, tap_row)
        for tap_col in range(3):
            tap = 8 - (3 * tap_row + tap_col)
            term = mm(sideways(value, tap_col).astype(BF16), take_rows(weights[1], tap * BOT, BOT), NT)
            acc = term if acc is None else acc + term
    half1, half1r = r_("half1"), r_("half1r")
    half1[0], half1[1] = acc[:, :HALF], acc[:, HALF:]
    slot = links.slots()
    links.put(half1.at[other], half1r, partner, slot)
    advance(third)
    links.landed(half1r, slot)
    dy1, dp1 = r_("dy1"), r_("dp1")
    gain, bias = norm1
    for group, rng in seg_rows(2):
        value = half1[s, rng, :] + half1r[rng, :]
        dy1[rng, :] = value * slope(pre1[rng, :] * gain + bias)
    put_stats("t1", 2, *with_hat(dy1, pre1))
    sums = add_up("t1")
    vec[s, 2:3, 2 * HALF:3 * HALF] = sums[1:2, :] + sums[3:4, :]
    vec[s, 2:3, 3 * HALF:4 * HALF] = sums[0:1, :] + sums[2:3, :]
    vec[s, 3:8, :] = jnp.zeros((5, WIDE), F32)
    vec_slot = links.slots()
    links.put(vec.at[s], vec.at[s], partner, vec_slot)
    for group, rng in seg_rows(2):
        dp1[s, rng, :] = norm_back(sums, group, rng, dy1, pre1, gain * inv1[group]).astype(BF16)
    slot = links.slots()
    links.put(dp1.at[s], dp1.at[s], partner, slot)
    for part_index in range(4):
        cols = slice(part_index * BOT, (part_index + 1) * BOT)
        put_rows(grad_of(0), part_index * BOT, mm(x[:, cols], dp1[s], TN).astype(BF16))
    first = reduced(0)
    advance(second)

    result = r_("dk_o")
    done_slot, done_out = links.slots(TAPS), links.outs(TAPS)

    def finish_unit(index):
        mine, _, _, _ = unit_at(index)
        final = lambda: links.copy(result.at[index], result.at[index], partner, done_out + index, done_slot + index)

        @pl.when(mine)
        def _():
            several(teams, lambda t: links.landed(dkg.at[0, 0], grad_slot + t * TAPS + index))
            acc = dkg[0, index].astype(F32)
            for number in range(1, teams):
                acc = acc + dkg[number, index].astype(F32)
            result[index] = acc.astype(BF16)
            final().start()

        return mine, final

    proj_done = line_sum("pj", proj_near())

    links.landed(r_("wback"), back_slot)
    links.landed(dp1.at[other], slot)
    value = mm(dp1[s], rows_half(s)[...].reshape(WIDE, HALF), NT)
    value = value + mm(dp1[other], r_("wback")[...].reshape(WIDE, HALF), NT) + du[...]
    for line in range(2):
        r_("small_grad_o")[line * WS:(line + 1) * WS, :] = value[line * LINE:line * LINE + WS, :]
        r_("large_grad_o")[line * WL:(line + 1) * WL, :] = value[line * LINE + WS:(line + 1) * LINE, :]
    advance(third)
    advance(first)
    advance(second)
    advance(first)
    advance(third)
    lax.fori_loop(0, TAPS, lambda i, c: (finish_unit(i), c)[1], 0)
    advance(second)

    def finished(index):
        mine, _, _, _ = unit_at(index)
        final = links.copy(result.at[index], result.at[index], partner, done_out + index, done_slot + index)
        pl.when(mine)(lambda: final.wait_send())
        pl.when(jnp.logical_not(mine))(lambda: links.landed(result.at[index], done_slot + index))

    advance(first)
    advance(second)
    advance(first)
    lax.fori_loop(0, TAPS, lambda i, c: (finished(i), c)[1], 0)
    r_("proj_o")[...] = proj_done()
    links.landed(vec.at[other], vec_slot)
    for index, out_part in enumerate(out_parts):
        links.landed(out_part, out_slot + index)
    links.close()
    used["send"], used["recv"] = links.used_send, links.used_recv


def body(
    reduce_weight,
    dilated_weight,
    expand_weight,
    reduce_gain,
    reduce_bias,
    dilated_gain,
    dilated_bias,
    expand_gain,
    expand_bias,
    head_conv,
    head_gain,
    head_bias,
    seg_proj,
    depth_proj,
    normal_proj,
    small_feats,
    small_labels,
    small_depth,
    small_normals,
    small_depth_valid,
    small_normal_valid,
    large_feats,
    large_labels,
    large_depth,
    large_normals,
    large_depth_valid,
    large_normal_valid,
):
    dp = lax.axis_size("dp")
    section = lax.axis_index("section")
    assert small_feats.shape[0] == 2 * WS and large_feats.shape[0] == 2 * WL
    shape = Shapes(dp)

    if not shape.inside:
        def whole(shard, wide):
            mine = lax.dynamic_slice_in_dim(shard, section * wide, wide, 1)
            return lax.all_gather(mine, "dp", axis=0, tiled=True)

        reduce_weight = whole(reduce_weight, HALF)
        dilated_weight = whole(dilated_weight, HALF)
        expand_weight = whole(expand_weight, WIDE)

    vmem = pl.BlockSpec(memory_space=pltpu.VMEM)
    anywhere = pl.BlockSpec(memory_space=pl.ANY)
    flat = lambda value: value.reshape(1, -1)
    inputs = {
        "reduce_w": reduce_weight,
        "dilated_w": dilated_weight,
        "expand_w": expand_weight,
        "head_w": head_conv.reshape(TAPS, shape.unit, HEADS),
        "reduce_gain": flat(reduce_gain),
        "reduce_bias": flat(reduce_bias),
        "dilated_gain": flat(dilated_gain),
        "dilated_bias": flat(dilated_bias),
        "expand_gain": flat(expand_gain),
        "expand_bias": flat(expand_bias),
        "head_gain": head_gain.reshape(-1, 128),
        "head_bias": head_bias.reshape(-1, 128),
        "seg_proj": seg_proj.T,
        "depth_proj": depth_proj.T,
        "normal_proj": normal_proj.T,
        "small_feats": small_feats,
        "small_labels": flat(small_labels),
        "small_depth": flat(small_depth),
        "small_normals": small_normals,
        "small_depth_valid": flat(small_depth_valid),
        "small_normal_valid": flat(small_normal_valid),
        "large_feats": large_feats,
        "large_labels": flat(large_labels),
        "large_depth": flat(large_depth),
        "large_normals": large_normals,
        "large_depth_valid": flat(large_depth_valid),
        "large_normal_valid": flat(large_normal_valid),
    }
    outputs = {
        "small_out_o": ((2 * WS, C), BF16),
        "large_out_o": ((2 * WL, C), BF16),
        "small_grad_o": ((2 * WS, WIDE), F32),
        "large_grad_o": ((2 * WL, WIDE), F32),
        "dk_o": ((TAPS, shape.unit, HEADS), BF16),
        "vec_o": ((2, 8, WIDE), F32),
        "head_vec_o": ((4, HEADS), F32),
        "proj_o": ((PROJ, HEADW), F32),
    }
    for index in range(3):
        if shape.inside:
            outputs[f"dw{index}_o"] = ((shape.rows[index], 2 * shape.wide[index]), BF16)
        else:
            outputs[f"dw{index}_o"] = ((shape.full[index], shape.wide[index]), BF16)
    scratch = scratch_of(shape)
    scratch["dscore"] = ((PROJ, LINE), F32)
    names = [*inputs, *outputs, *scratch, "send", "recv"]
    used = {}

    def call(room, *operands):
        return pl.pallas_call(
            functools.partial(fused, shape, names, used),
            out_shape=[jax.ShapeDtypeStruct(dims, kind) for dims, kind in outputs.values()],
            in_specs=[anywhere if name == "head_w" else vmem for name in inputs],
            out_specs=[vmem] * len(outputs),
            scratch_shapes=[pltpu.VMEM(dims, kind) for dims, kind in scratch.values()]
            + [pltpu.SemaphoreType.DMA((count,)) for count in room],
            compiler_params=pltpu.CompilerParams(
                collective_id=0, has_side_effects=True, vmem_limit_bytes=64 * 2**20 - 2**16
            ),
            name="fused",
        )(*operands)

    jax.eval_shape(functools.partial(call, (2048, 2048)), *inputs.values())
    got = dict(zip(outputs, call((used["send"], used["recv"]), *inputs.values())))
    if not shape.inside:
        for index in range(3):
            mine = lax.psum_scatter(got[f"dw{index}_o"].astype(F32), "dp", scatter_dimension=0, tiled=True)
            both = lax.all_gather(mine, "section", axis=0)
            got[f"dw{index}_o"] = both.transpose(1, 0, 2).reshape(shape.rows[index], -1)

    results = {
        "small_out": ((2 * WS, C), BF16),
        "large_out": ((2 * WL, C), BF16),
        "small_grad": ((2 * WS, WIDE), F32),
        "large_grad": ((2 * WL, WIDE), F32),
        "dw0": ((shape.rows[0], BOT), F32),
        "dw1": ((shape.rows[1], BOT), F32),
        "dw2": ((shape.rows[2], C), F32),
        "reduce_gain": ((1, BOT), F32),
        "reduce_bias": ((1, BOT), F32),
        "dilated_gain": ((1, BOT), F32),
        "dilated_bias": ((1, BOT), F32),
        "expand_gain": ((1, C), F32),
        "expand_bias": ((1, C), F32),
        "dk": ((TAPS * shape.unit, HEADS), F32),
        "head_gain": ((HEADS // 128, 128), F32),
        "head_bias": ((HEADS // 128, 128), F32),
        "seg_proj": ((NCLS, HEADW), F32),
        "depth_proj": ((1, HEADW), F32),
        "normal_proj": ((3, HEADW), F32),
    }
    final = pl.pallas_call(
        functools.partial(finish, [*got, *results]),
        out_shape=[jax.ShapeDtypeStruct(dims, kind) for dims, kind in results.values()],
        in_specs=[vmem] * len(got),
        out_specs=[vmem] * len(results),
        compiler_params=pltpu.CompilerParams(vmem_limit_bytes=64 * 2**20 - 2**16),
        name="finish",
    )(*got.values())
    vectors = ("gain", "bias")
    return tuple(
        value.reshape(-1) if name.endswith(vectors) else value.T if name.endswith("proj") else value
        for name, value in zip(results, final)
    )


def finish(names, *refs):
    env = dict(zip(names, refs))
    for name in ("small_out", "large_out", "small_grad", "large_grad"):
        env[name][...] = env[name + "_o"][...]
    for index in range(3):
        env[f"dw{index}"][...] = env[f"dw{index}_o"][...].astype(F32)
    taps, unit, _ = env["dk_o"].shape
    for tap in range(taps):
        env["dk"][tap * unit:(tap + 1) * unit, :] = env["dk_o"][tap].astype(F32)
    vec, head_vec = env["vec_o"], env["head_vec_o"]
    for section in range(2):
        for row, name in enumerate(("expand_gain", "expand_bias")):
            env[name][0:1, section * WIDE:(section + 1) * WIDE] = vec[section, row:row + 1, :]
        for part, name in enumerate(("dilated_gain", "dilated_bias", "reduce_gain", "reduce_bias")):
            env[name][0:1, section * HALF:(section + 1) * HALF] = vec[section, 2:3, part * HALF:(part + 1) * HALF]
    gain = head_vec[1:2, :] + head_vec[3:4, :]
    bias = head_vec[0:1, :] + head_vec[2:3, :]
    for part in range(HEADS // 128):
        cols = slice(part * 128, (part + 1) * 128)
        env["head_gain"][part:part + 1, :] = gain[:, cols]
        env["head_bias"][part:part + 1, :] = bias[:, cols]
    proj = env["proj_o"]
    env["seg_proj"][...] = proj[0:NCLS, :]
    env["depth_proj"][...] = proj[DEPTH_ROW:DEPTH_ROW + 1, :]
    env["normal_proj"][...] = proj[NORMAL_ROW:NORMAL_ROW + 3, :]


def solution(mesh):
    rows, vector = P("dp", None), P()
    pixels, parts = P("dp"), P(None, "dp")
    group = (rows, pixels, pixels, parts, pixels, pixels)
    in_specs = (rows, rows, rows) + (vector,) * 6 + (rows,) + (vector,) * 5 + group + group
    out_specs = (
        (rows, rows, P("dp", "section"), P("dp", "section"), rows, rows, rows)
        + (vector,) * 6
        + (rows,)
        + (vector,) * 5
    )
    return jax.shard_map(body, mesh=mesh, in_specs=in_specs, out_specs=out_specs, check_vma=False)
```

```python
import functools

import jax
import jax.numpy as jnp
from jax import lax
from jax.experimental import pallas as pl
from jax.experimental.pallas import tpu as pltpu
from jax.sharding import PartitionSpec as P

C = 2048
BOT = 512
HEADW = 256
NCLS = 13
WS = 48
WL = 80
HS = 36
HL = 60

EPS = 1e-05
RIDGE = 0.1
SWEEPS = 5

F32 = jnp.float32
BF16 = jnp.bfloat16
MESH = pl.DeviceIdType.MESH

LINE = WS + WL
SEGMENTS = ((0, WS), (WS, WL))
HEIGHTS = (HS, HL)
PIX = 2 * LINE
TEAM = 8
CH = C // TEAM
HALF = BOT // 2
WIDE = C // 2
HEADS = 3 * HEADW
TAPS = 9
PROJ = 32
DEPTH_ROW = 16
NORMAL_ROW = 24

NN = (((1,), (0,)), ((), ()))
NT = (((1,), (1,)), ((), ()))
TN = (((0,), (0,)), ((), ()))


def mm(left, right, dims=NN):
    return lax.dot_general(left, right, dims, preferred_element_type=F32)


def flip(rank, bits):
    out = rank
    for bit in (1, 2, 4):
        if bits & bit:
            out = out + bit * (1 - 2 * ((rank // bit) % 2))
    return out


def sigmoid(value):
    return 1.0 / (1.0 + jnp.exp(-value))


def silu(value):
    return value * sigmoid(value)


def slope(value):
    sigma = sigmoid(value)
    return sigma * (1.0 + value * (1.0 - sigma))


def seg_rows(lines):
    for line in range(lines):
        for group, (start, length) in enumerate(SEGMENTS):
            yield group, slice(line * LINE + start, line * LINE + start + length)


def position(rows):
    return lax.broadcasted_iota(jnp.int32, (rows, 1), 0) % LINE


def column_mask(rows, tap_col):
    place = position(rows)
    small = place < WS
    column = jnp.where(small, place, place - WS) + (2 * tap_col - 2)
    width = jnp.where(small, WS, WL)
    return ((column >= 0) & (column < width)).astype(F32)


def sideways(value, tap_col):
    rows = value.shape[0]
    if tap_col == 1:
        return value
    return pltpu.roll(value, (2 - 2 * tap_col) % rows, 0) * column_mask(rows, tap_col)


def jacobi_weights(gram):
    third = (gram[0, 0] + gram[1, 1] + gram[2, 2]) / 3.0 * RIDGE
    matrix = {(i, j): gram[min(i, j), max(i, j)] + (third if i == j else 0.0) for i in range(3) for j in range(3)}
    one, zero = jnp.ones_like(third), jnp.zeros_like(third)
    vectors = {(i, j): one if i == j else zero for i in range(3) for j in range(3)}
    for _ in range(SWEEPS):
        for p, q in ((0, 1), (0, 2), (1, 2)):
            up = 2.0 * matrix[p, q]
            across = matrix[q, q] - matrix[p, p]
            scale = jnp.maximum(jnp.abs(up), jnp.abs(across))
            still = scale == 0.0
            scale = jnp.where(still, 1.0, scale)
            up, across = up / scale, across / scale
            length = jnp.where(still, 1.0, jnp.sqrt(up * up + across * across))
            larger = jnp.sqrt(0.5 + 0.5 * jnp.abs(across) / length)
            smaller = 0.5 * up / (length * larger)
            sign = jnp.where(up < 0.0, -1.0, 1.0)
            cosine = jnp.where(still, 1.0, jnp.where(across >= 0.0, larger, jnp.abs(smaller)))
            sine = jnp.where(still, 0.0, jnp.where(across >= 0.0, smaller, sign * larger))
            for i in range(3):
                first, second = matrix[i, p], matrix[i, q]
                matrix[i, p] = first * cosine - second * sine
                matrix[i, q] = first * sine + second * cosine
                first, second = vectors[i, p], vectors[i, q]
                vectors[i, p] = first * cosine - second * sine
                vectors[i, q] = first * sine + second * cosine
            for j in range(3):
                first, second = matrix[p, j], matrix[q, j]
                matrix[p, j] = first * cosine - second * sine
                matrix[q, j] = first * sine + second * cosine
    values = [matrix[i, i] for i in range(3)]
    least = jnp.sqrt(jnp.minimum(jnp.minimum(values[0], values[1]), values[2]))
    alphas = []
    roots = [lax.rsqrt(value) for value in values]
    sums = [vectors[0, k] + vectors[1, k] + vectors[2, k] for k in range(3)]
    for t in range(3):
        alphas.append(least * sum(vectors[t, k] * roots[k] * sums[k] for k in range(3)))
    return alphas


class Links:
    def __init__(self, send, recv, partner):
        self.send, self.recv, self.partner = send, recv, partner
        self.used_send = self.used_recv = 0
        self.open = []

    def slots(self, count=1):
        first = self.used_recv
        self.used_recv += count
        assert self.used_recv <= self.recv.shape[0]
        return first

    def outs(self, count=1):
        first = self.used_send
        self.used_send += count
        assert self.used_send <= self.send.shape[0]
        return first

    def copy(self, src, dst, device, out, slot):
        return pltpu.make_async_remote_copy(
            src_ref=src, dst_ref=dst, send_sem=self.send.at[out], recv_sem=self.recv.at[slot],
            device_id=device, device_id_type=MESH,
        )

    def put(self, src, dst, device, slot, when=None):
        out = self.outs()
        if when is not None:
            device = tuple(jnp.where(when, to, near) for to, near in zip(device, self.partner))
        make = functools.partial(self.copy, src, dst, device, out, slot)
        if when is None:
            make().start()
            done = lambda: make().wait_send()
        else:
            pl.when(when)(lambda: make().start())
            done = lambda: pl.when(when)(lambda: make().wait_send())
        self.open.append(done)
        return done

    def put_or_keep(self, src, dst, device, slot, mine, when=True):
        pl.when(when & mine)(lambda: pltpu.make_async_copy(src, dst, self.recv.at[slot]).start())
        return self.put(src, dst, device, slot, when & jnp.logical_not(mine))

    def landed(self, dst, slot, when=None):
        wait = lambda: pltpu.make_async_copy(dst, dst, self.recv.at[slot]).wait()
        if when is None:
            wait()
        else:
            pl.when(when)(wait)

    def close(self):
        for done in self.open:
            done()
        self.open = []


def pieces(ref, start, count):
    rows = ref.shape[2]
    at = start
    while at < start + count:
        shard, first = at // rows, at % rows
        length = min(rows - first, start + count - at)
        yield (shard // 4, shard % 4, slice(first, first + length)), slice(at - start, at - start + length)
        at += length


def take_rows(ref, start, count):
    if len(ref.shape) == 2:
        return ref[start:start + count, :]
    found = [ref[(*place, slice(None))] for place, _ in pieces(ref, start, count)]
    return found[0] if len(found) == 1 else jnp.concatenate(found, axis=0)


def put_rows(ref, start, value):
    if len(ref.shape) == 2:
        ref[start:start + value.shape[0], :] = value
        return
    for place, rows in pieces(ref, start, value.shape[0]):
        ref[(*place, slice(None))] = value[rows, :]


def several(count, body):
    if count <= 4:
        for index in range(count):
            body(index)
    else:
        lax.fori_loop(0, count, lambda index, carry: (body(index), carry)[1], 0)


class Shapes:
    def __init__(self, dp):
        self.dp = dp
        self.planes = dp // 4
        self.teams = dp // TEAM
        self.unit = C // dp
        self.units_half = dp // (2 * TEAM)
        self.rows = (C // dp, TAPS * BOT // dp, BOT // dp)
        self.wide = (HALF, HALF, WIDE)
        self.full = (C, TAPS * BOT, BOT)
        self.inside = all(rows % 32 == 0 for rows in self.rows)
        self.borders = 2 * dp > min(HEIGHTS)


def scratch_of(shape):
    planes = shape.planes
    table = {
        "x": ((PIX, C), BF16),
        "xh": ((PIX, WIDE), BF16),
        "wback": ((planes // 2, 4, C // shape.dp, HALF) if shape.inside else (WIDE, HALF), BF16),
        "kernel": ((TAPS, 2, CH // 2, HEADS), BF16),
        "pre1": ((PIX, HALF), F32),
        "pre2": ((PIX, HALF), F32),
        "pre3": ((PIX, WIDE), F32),
        "act1": ((3, 2, PIX, HALF), BF16),
        "act1s": ((3, 3, 2, PIX, HALF), BF16),
        "patch2": ((PIX, TAPS * BOT), BF16),
        "act2": ((2, PIX, HALF), BF16),
        "outb": ((4, 2, PIX, CH // 2), BF16),
        "outs": ((3, 6, 2, PIX, CH // 2), BF16),
        "patch": ((PIX, TAPS * CH), BF16),
        "part": ((8, LINE, HEADS), BF16),
        "partm": ((8, 8, HEADS), F32),
        "parts": ((TEAM, LINE, HEADS), BF16),
        "partsm": ((TEAM, 8, HEADS), F32),
        "preh": ((LINE, HEADS), F32),
        "acth": ((LINE, HEADS), BF16),
        "dyh": ((LINE, HEADS), F32),
        "dph": ((LINE, HEADS), BF16),
        "dpx": ((6, 2, LINE, HEADS), BF16),
        "dps": ((3, 6, PIX, HEADW), BF16),
        "grads": ((3, 4, PIX, CH), F32),
        "doutb": ((4, PIX, CH), BF16),
        "dout": ((4, PIX, CH), BF16),
        "du": ((PIX, WIDE), F32),
        "dpre3": ((PIX, WIDE), BF16),
        "half2": ((2, PIX, HALF), F32),
        "half2r": ((PIX, HALF), F32),
        "dy2": ((PIX, HALF), F32),
        "dp2": ((3, PIX, HALF), BF16),
        "half1": ((2, PIX, HALF), F32),
        "half1r": ((PIX, HALF), F32),
        "dy1": ((PIX, HALF), F32),
        "dp1": ((2, PIX, HALF), BF16),
        "dks": ((TAPS, CH // 2, HEADS), BF16),
        "dkr": ((TAPS, CH // 2, HEADS), BF16),
        "dku": ((TAPS, CH // 2, HEADS), BF16),
        "dproj": ((PROJ, HEADW), F32),
        "head_norm": ((8, HEADS), F32),
        "tallies": ((4, LINE), F32),
        "marks": ((8, LINE), jnp.int32),
        "values": ((16, LINE), F32),
        "proj": ((PROJ, HEADS), BF16),
        "dkg": ((shape.teams, TAPS, shape.unit, HEADS), BF16),
    }
    for name, count, width in (
        ("s1", 4, HALF), ("s2", 4, HALF), ("s3", 4, WIDE), ("t3", 4, WIDE), ("t2", 4, HALF), ("t1", 4, HALF),
        ("sh", 8, HEADS), ("th", 8, HEADS),
    ):
        rows = 8 if name == "s1" else 4
        table[name + "a"] = ((count, rows, width), F32)
        table[name + "b"] = ((planes, rows, width), F32)
    for name, rows, width in (("gm", 8, 128), ("pj", PROJ, HEADW)):
        table[name + "a"] = ((8, rows, width), F32)
        table[name + "b"] = ((planes, rows, width), F32)
    for index in range(3):
        rows, wide = shape.rows[index], shape.wide[index]
        if shape.inside:
            table[f"w{index}"] = ((planes, 4, rows, wide), BF16)
            table[f"dw{index}"] = ((planes, 4, rows, wide), BF16)
            table[f"ra{index}"] = ((2, planes, 2, rows // 2, wide), BF16)
            table[f"rb{index}"] = ((2, planes, rows // 2, wide), BF16)
            table[f"rc{index}"] = ((planes, rows, wide), BF16)
    return table


def fused(shape, names, used, *refs):
    env = dict(zip(names, refs))
    r_ = lambda name: env[name]
    s = lax.axis_index("section")
    d = lax.axis_index("dp")
    dp, planes, teams = shape.dp, shape.planes, shape.teams
    other = 1 - s
    plane, spot = d // 4, d % 4
    team, rank = d // TEAM, d % TEAM
    partner = (other, d)
    links = Links(r_("send"), r_("recv"), partner)

    gate = pltpu.get_barrier_semaphore()
    total = 2 * dp
    me = s * dp + d

    def greet(offset, carry):
        to = (me + offset) % total
        pl.semaphore_signal(gate, inc=1, device_id=(to // dp, to % dp), device_id_type=MESH)
        return carry

    lax.fori_loop(1, total, greet, 0)

    x = r_("x")
    for line in range(2):
        x[line * LINE:line * LINE + WS, :] = r_("small_feats")[line * WS:(line + 1) * WS, :]
        x[line * LINE + WS:(line + 1) * LINE, :] = r_("large_feats")[line * WL:(line + 1) * WL, :]
    marks, values, proj = r_("marks"), r_("values"), r_("proj")
    head_norm = r_("head_norm")
    for row, name in enumerate(("head_gain", "head_bias")):
        for part in range(HEADS // 128):
            head_norm[row:row + 1, part * 128:(part + 1) * 128] = r_(name)[part:part + 1, :]

    def own_line(section):
        small, large = slice(section * WS, (section + 1) * WS), slice(section * WL, (section + 1) * WL)
        for row, name in enumerate(("labels", "depth_valid", "normal_valid")):
            marks[row:row + 1, 0:WS] = r_("small_" + name)[:, small]
            marks[row:row + 1, WS:LINE] = r_("large_" + name)[:, large]
        for row, count, name in ((0, 1, "depth"), (8, 3, "normals")):
            values[row:row + count, 0:WS] = r_("small_" + name)[:, small]
            values[row:row + count, WS:LINE] = r_("large_" + name)[:, large]

    for section in range(2):
        pl.when(s == section)(functools.partial(own_line, section))
    proj[...] = jnp.zeros(proj.shape, BF16)
    for task, (row, name) in enumerate(((0, "seg_proj"), (DEPTH_ROW, "depth_proj"), (NORMAL_ROW, "normal_proj"))):
        matrix = r_(name)[...]
        proj[row:row + matrix.shape[0], task * HEADW:(task + 1) * HEADW] = matrix
    xh = r_("xh")
    xh_slot = links.slots()
    pltpu.make_async_copy(x.at[:, pl.ds(pl.multiple_of(s * WIDE, WIDE), WIDE)], xh, links.recv.at[xh_slot]).start()
    pl.semaphore_wait(gate, total - 1)

    def plane_sum(key, width_of):
        near = r_(key + "a")
        count = near.shape[0]
        own = spot if count == 4 else 4 * s + spot
        first = links.slots(count)
        for bits in range(1, count):
            to = flip(own, bits)
            device = (s, 4 * plane + to) if count == 4 else (to // 4, 4 * plane + to % 4)
            links.put(near.at[own], near.at[own], device, first + bits)

        def finish():
            for bits in range(1, count):
                links.landed(near.at[flip(own, bits)], first + bits)
            acc = near[0]
            for index in range(1, count):
                acc = acc + near[index]
            return acc

        return finish

    def line_sum(key, value):
        far = r_(key + "b")
        far[plane] = value
        first, out = links.slots(planes), links.outs(planes)

        def make(offset):
            to = (plane + offset) % planes
            return links.copy(far.at[plane], far.at[plane], (s, 4 * to + spot), out + offset, first + offset)

        several(planes - 1, lambda i: make(i + 1).start())
        links.open.append(lambda: several(planes - 1, lambda i: make(i + 1).wait_send()))

        def finish():
            several(planes - 1, lambda i: links.landed(far.at[0], first + i + 1))
            acc = far[0]
            for index in range(1, planes):
                acc = acc + far[index]
            return acc

        return finish

    def add_up(key):
        return line_sum(key, plane_sum(key, None)())()

    def own_slot(key):
        near = r_(key + "a")
        return near.at[spot if near.shape[0] == 4 else 4 * s + spot]

    def put_stats(key, rows, first, second=None):
        slot = own_slot(key)
        for group in range(2):
            a = b = None
            for g, rng in seg_rows(rows):
                if g == group:
                    one, two = first(g, rng), second(g, rng)
                    one, two = jnp.sum(one, axis=0, keepdims=True), jnp.sum(two, axis=0, keepdims=True)
                    a, b = (one, two) if a is None else (a + one, b + two)
            slot[2 * group:2 * group + 1, :] = a
            slot[2 * group + 1:2 * group + 2, :] = b

    counts = (2.0 * dp * WS, 2.0 * dp * WL)

    def moments(sums):
        means, invs = [], []
        for group in range(2):
            mean = sums[2 * group:2 * group + 1, :] / counts[group]
            var = sums[2 * group + 1:2 * group + 2, :] / counts[group] - mean * mean
            means.append(mean)
            invs.append(lax.rsqrt(var + EPS))
        return means, invs

    gathers = []
    if shape.inside:
        shards = (
            r_("reduce_w").at[:, pl.ds(pl.multiple_of(s * HALF, HALF), HALF)],
            r_("dilated_w").at[:, pl.ds(pl.multiple_of(s * HALF, HALF), HALF)],
            r_("expand_w").at[:, pl.ds(pl.multiple_of(s * WIDE, WIDE), WIDE)],
        )
        near_x, near_y, corner = flip(spot, 1), flip(spot, 2), flip(spot, 3)
        at_x, at_y = (s, 4 * plane + near_x), (s, 4 * plane + near_y)

        def gather(index):
            rows, wide = shape.rows[index], shape.wide[index]
            buf = r_(f"w{index}")
            cut = rows // 2
            first, out = links.slots(planes), links.outs(planes)
            mine = pltpu.make_async_copy(shards[index], buf.at[plane, spot], links.recv.at[first])
            mine.start()

            def make(offset):
                to = (plane + offset) % planes
                return links.copy(shards[index], buf.at[plane, spot], (s, 4 * to + spot), out + offset, first + offset)

            several(planes - 1, lambda i: make(i + 1).start())
            links.open.append(lambda: several(planes - 1, lambda i: make(i + 1).wait_send()))
            up, low = pl.ds(0, cut), pl.ds(cut, cut)
            slot = links.slots(6)
            yield
            mine.wait()
            several(planes - 1, lambda i: links.landed(buf.at[0, 0], first + i + 1))
            links.put(buf.at[:, spot, up], buf.at[:, spot, up], at_x, slot)
            links.put(buf.at[:, spot, low], buf.at[:, spot, low], at_y, slot + 1)
            links.put(buf.at[:, spot, up], buf.at[:, spot, up], at_y, slot + 2)
            links.put(buf.at[:, spot, low], buf.at[:, spot, low], at_x, slot + 3)
            yield
            links.landed(buf.at[:, near_x, up], slot)
            links.put(buf.at[:, near_x, up], buf.at[:, near_x, up], at_y, slot + 4)
            links.landed(buf.at[:, near_y, low], slot + 1)
            links.put(buf.at[:, near_y, low], buf.at[:, near_y, low], at_x, slot + 5)
            yield
            links.landed(buf.at[:, near_y, up], slot + 2)
            links.landed(buf.at[:, near_x, low], slot + 3)
            links.landed(buf.at[:, corner, up], slot + 4)
            links.landed(buf.at[:, corner, low], slot + 5)
            yield

        gathers = [gather(index) for index in range(3)]
        for one in gathers:
            next(one)
        weights = [r_(f"w{index}") for index in range(3)]
    else:
        weights = [r_("reduce_w"), r_("dilated_w"), r_("expand_w")]

    def gather_on(index):
        if shape.inside:
            next(gathers[index])

    kernel = r_("kernel")
    unit, halves = shape.unit, shape.units_half
    share = 2 * halves
    kernel_slot = links.slots(TAPS * halves)
    kernel_out = links.outs(TAPS * teams)

    def unit_at(index):
        number = TAPS * d + index
        tap, chunk = number // dp, number % dp
        inner = chunk % share
        return inner // halves == s, chunk // share, tap, inner % halves

    def kernel_copy(index, to_team):
        sends, to_rank, tap, place = unit_at(index)
        src = r_("head_w").at[index]
        dst = kernel.at[tap, s, pl.ds(pl.multiple_of(place * unit, unit), unit)]
        to = to_team * TEAM + to_rank
        slot = kernel_slot + tap * halves + place
        to_core = jnp.where(to == d, other, s)
        remote = lambda: links.copy(src, dst, (to_core, to), kernel_out + index * teams + to_team, slot)
        local = lambda: pltpu.make_async_copy(src, dst, links.recv.at[slot])
        return sends, to == d, remote, local

    def kernel_start(index, to_team):
        sends, mine, remote, local = kernel_copy(index, to_team)
        pl.when(sends & mine)(lambda: local().start())
        pl.when(sends & jnp.logical_not(mine))(lambda: remote().start())

    def kernel_done(index, to_team):
        sends, mine, remote, _ = kernel_copy(index, to_team)
        pl.when(sends & jnp.logical_not(mine))(lambda: remote().wait_send())

    def kernel_send():
        lax.fori_loop(0, TAPS * teams, lambda i, c: (kernel_start(i // teams, i % teams), c)[1], 0)

    links.open.append(lambda: lax.fori_loop(0, TAPS * teams, lambda i, c: (kernel_done(i // teams, i % teams), c)[1], 0))

    def same_image(block, tap_row):
        near = block + (tap_row - 1)
        inside = (near >= 0) & (near < dp)
        return [inside & ((2 * near + 2 * height) // height == (2 * block + 2 * height) // height) for height in HEIGHTS]

    def row_mask(block, tap_row, rows=PIX):
        small, large = [flag.astype(F32) for flag in same_image(block, tap_row)]
        return jnp.where(position(rows) < WS, small, large)

    def own_part(name, width):
        return r_(name)[0:1, pl.ds(pl.multiple_of(s * width, width), width)]

    norm1 = own_part("reduce_gain", HALF), own_part("reduce_bias", HALF)
    norm2 = own_part("dilated_gain", HALF), own_part("dilated_bias", HALF)
    norm3 = own_part("expand_gain", WIDE), own_part("expand_bias", WIDE)
    pre1, pre2, pre3 = r_("pre1"), r_("pre2"), r_("pre3")
    act1, act2 = r_("act1"), r_("act2")
    squares = lambda ref: (lambda g, rng: ref[rng, :], lambda g, rng: ref[rng, :] * ref[rng, :])

    gather_on(0)
    gather_on(0)
    gather_on(1)
    kernel_send()
    gather_on(0)
    pre1[...] = mm(x[...], take_rows(weights[0], 0, C))
    back_slot = links.slots()
    half_planes = planes // 2

    def rows_half(section):
        if shape.inside:
            return weights[0].at[pl.ds(pl.multiple_of(section * half_planes, half_planes), half_planes)]
        return weights[0].at[pl.ds(pl.multiple_of(section * WIDE, WIDE), WIDE)]

    links.put(rows_half(other), r_("wback"), partner, back_slot)
    put_stats("s1", 2, *squares(pre1))
    slot_ref = own_slot("s1")
    slot_ref[4:8, :] = jnp.zeros((4, HALF), F32)
    lane = lax.broadcasted_iota(jnp.int32, (1, LINE), 1)
    tally = jnp.zeros((1, LINE), F32)
    for number, name in enumerate(("labels", "depth_valid", "normal_valid")):
        for group, size in enumerate(("small_", "large_")):
            value = r_(size + name)[...]
            keep = (value >= 0).astype(F32) if number == 0 else value.astype(F32)
            count = jnp.sum(keep, axis=1, keepdims=True)
            tally = tally + jnp.where(lane == 2 * number + group, count, 0.0)
    slot_ref[4:5, 0:LINE] = tally
    gather_on(1)
    gather_on(2)
    sums = add_up("s1")
    mean1, inv1 = moments(sums)
    tallies = r_("tallies")
    tallies[...] = sums[4:8, 0:LINE]
    gain, bias = norm1
    for group, rng in seg_rows(2):
        hat = (pre1[rng, :] - mean1[group]) * inv1[group]
        pre1[rng, :] = hat
        act1[1, s, rng, :] = silu(hat * gain + bias).astype(BF16)
    slot = links.slots(5)
    above, below = jnp.maximum(d - 1, 0), jnp.minimum(d + 1, dp - 1)
    has_above, has_below = d > 0, d < dp - 1
    links.put(act1.at[1, s], act1.at[2, s], (s, above), slot + 1 + s, has_above)
    links.put(act1.at[1, s], act1.at[0, s], (s, below), slot + 3 + s, has_below)
    links.put(act1.at[1, s], act1.at[1, s], partner, slot)

    @pl.when(jnp.logical_not(has_above))
    def _():
        act1[0] = jnp.zeros(act1.shape[1:], BF16)

    @pl.when(jnp.logical_not(has_below))
    def _():
        act1[2] = jnp.zeros(act1.shape[1:], BF16)

    act1s, patch2 = r_("act1s"), r_("patch2")
    gather_on(2)

    def spread_rows(tap_row, half):
        value = act1[tap_row, half].astype(F32)
        if tap_row != 1 and shape.borders:
            value = value * row_mask(d, tap_row)
        for tap_col in range(3):
            piece = sideways(value, tap_col).astype(BF16)
            at = (3 * tap_row + tap_col) * BOT + half * HALF
            act1s[tap_col, tap_row, half] = piece
            patch2[:, at:at + HALF] = piece

    links.landed(act1.at[1, other], slot)
    for half in range(2):
        spread_rows(1, half)
    links.landed(act1.at[2, s], slot + 1 + s, has_below)
    links.put(act1.at[2, s], act1.at[2, s], partner, slot + 1 + s, has_below)
    links.landed(act1.at[0, s], slot + 3 + s, has_above)
    links.put(act1.at[0, s], act1.at[0, s], partner, slot + 3 + s, has_above)
    links.landed(act1.at[2, other], slot + 1 + other, has_below)
    for half in range(2):
        spread_rows(2, half)
    links.landed(act1.at[0, other], slot + 3 + other, has_above)
    for half in range(2):
        spread_rows(0, half)
    gather_on(1)
    pre2[...] = mm(patch2[...], take_rows(weights[1], 0, TAPS * BOT))
    put_stats("s2", 2, *squares(pre2))
    mean2, inv2 = moments(add_up("s2"))
    gain, bias = norm2
    for group, rng in seg_rows(2):
        hat = (pre2[rng, :] - mean2[group]) * inv2[group]
        pre2[rng, :] = hat
        act2[s, rng, :] = silu(hat * gain + bias).astype(BF16)
    slot = links.slots()
    links.put(act2.at[s], act2.at[s], partner, slot)
    gather_on(2)
    links.landed(act2.at[other], slot)
    pre3[...] = mm(act2[0], take_rows(weights[2], 0, HALF)) + mm(act2[1], take_rows(weights[2], HALF, HALF))
    put_stats("s3", 2, *squares(pre3))
    mean3, inv3 = moments(add_up("s3"))
    links.landed(xh, xh_slot)
    gain, bias = norm3
    outb = r_("outb")
    for group, rng in seg_rows(2):
        hat = (pre3[rng, :] - mean3[group]) * inv3[group]
        pre3[rng, :] = hat
        value = silu(hat * gain + bias + xh[rng, :].astype(F32)).astype(BF16)
        for part in range(4):
            for half in range(2):
                at = part * CH + half * (CH // 2)
                outb[part, half, rng, :] = value[:, at:at + CH // 2]
        start, length = SEGMENTS[group]
        line = rng.start // LINE
        whole = r_(("small_out_o", "large_out_o")[group])
        whole[line * length:(line + 1) * length, pl.ds(pl.multiple_of(s * WIDE, WIDE), WIDE)] = value

    outs = r_("outs")
    seat = rank // 4
    slot = links.slots(6)
    for part in range(4):
        to_rank = 4 * s + part
        src = outb.at[part]
        chip = team * TEAM + to_rank
        links.put_or_keep(src, outs.at[1, rank % 4 + 1], (seat, chip), slot + rank % 4 + 1, (seat == s) & (part == rank % 4))
    out_slot = links.slots(2)
    out_parts = [r_(name).at[:, pl.ds(pl.multiple_of(s * WIDE, WIDE), WIDE)] for name in ("small_out_o", "large_out_o")]
    for index, out_part in enumerate(out_parts):
        links.put(out_part, out_part, partner, out_slot + index)
    has_low = (s == 1) | (team > 0)
    has_high = (s == 0) | (team < teams - 1)

    @pl.when(jnp.logical_not(has_low))
    def _():
        outs[1, 0] = jnp.zeros((2, PIX, CH // 2), BF16)

    @pl.when(jnp.logical_not(has_high))
    def _():
        outs[1, 5] = jnp.zeros((2, PIX, CH // 2), BF16)

    near_block, near_border = 4 - 3 * s, 5 * s
    far_block, far_border = 1 + 3 * s, 5 - 5 * s
    far_chip = (other, jnp.clip(d + TEAM * (2 * s - 1), 0, dp - 1))
    has_far = (has_low & (s == 0)) | (has_high & (s == 1))
    for index in range(1, 5):
        links.landed(outs.at[1, index], slot + index)
    links.put(outs.at[1, near_block], outs.at[1, near_border], partner, slot + near_border)
    links.put(outs.at[1, far_block], outs.at[1, far_border], far_chip, slot + far_border, has_far)

    swap_slot = links.slots()
    several(TAPS * halves, lambda i: links.landed(kernel.at[0, 0, pl.ds(0, unit)], kernel_slot + i))
    links.put(kernel.at[:, s], kernel.at[:, s], partner, swap_slot)

    def widen(index, carry):
        for half in range(2):
            value = outs[1, index, half].astype(F32)
            outs[0, index, half] = sideways(value, 0).astype(BF16)
            outs[2, index, half] = sideways(value, 2).astype(BF16)
        return carry

    lax.fori_loop(1, 5, widen, 0)
    links.landed(kernel.at[:, other], swap_slot)

    first_block = team * TEAM + 4 * s
    patch, part, partm = r_("patch"), r_("part"), r_("partm")
    parts, partsm = r_("parts"), r_("partsm")
    part_slot = links.slots(2 * TEAM)

    def head_block(index):
        for tap_row in range(3):
            for tap_col in range(3):
                for half in range(2):
                    piece = outs[tap_col, index + tap_row, half]
                    if tap_row != 1 and shape.borders:
                        piece = piece * row_mask(first_block + index, tap_row).astype(BF16)
                    at = (3 * tap_row + tap_col) * CH + half * (CH // 2)
                    patch[:, at:at + CH // 2] = piece
        value = mm(patch[...], kernel[...].reshape(TAPS * CH, HEADS))
        for line in range(2):
            number = 2 * index + line
            for group, (start, length) in enumerate(SEGMENTS):
                rows = value[line * LINE + start:line * LINE + start + length, :]
                middle = jnp.mean(rows, axis=0, keepdims=True)
                partm[number, group:group + 1, :] = middle
                part[number, start:start + length, :] = (rows - middle).astype(BF16)
            chip = team * TEAM + 4 * s + index
            mine = (4 * s + index == rank) & (s == line)
            links.put_or_keep(part.at[number], parts.at[rank], (line, chip), part_slot + rank, mine)
            links.put_or_keep(partm.at[number], partsm.at[rank], (line, chip), part_slot + TEAM + rank, mine)

    head_block(1)
    head_block(2)
    links.landed(outs.at[1, 0], slot, has_low)
    links.landed(outs.at[1, 5], slot + 5, has_high)
    widen(0, 0)
    widen(5, 0)
    head_block(0)
    head_block(3)

    for index in range(TEAM):
        links.landed(parts.at[index], part_slot + index)
        links.landed(partsm.at[index], part_slot + TEAM + index)
    preh, acth, dyh = r_("preh"), r_("acth"), r_("dyh")
    for group, (start, length) in enumerate(SEGMENTS):
        rng = slice(start, start + length)
        acc = sum(parts[index, rng, :].astype(F32) for index in range(TEAM))
        acc = acc + sum(partsm[index, group:group + 1, :] for index in range(TEAM))
        preh[rng, :] = acc

    labels, depth, normals = marks[0:1, :], values[0:1, :], values[8:11, :]
    seg_keep = (labels >= 0).astype(F32)
    depth_keep, normal_keep = marks[1:2, :].astype(F32), marks[2:3, :].astype(F32)
    small_lane = lane < WS
    put_stats("sh", 1, *squares(preh))
    sums = add_up("sh")
    meanh, invh = moments(sums)
    tally = tallies[0:1, :]

    def pixel_count(number):
        picked = [jnp.sum(jnp.where(lane == 2 * number + group, tally, 0.0), axis=1, keepdims=True) for group in range(2)]
        return jnp.maximum(jnp.where(small_lane, picked[0], picked[1]), 1.0)

    gain, bias = head_norm[0:1, :], head_norm[1:2, :]
    for group, rng in seg_rows(1):
        hat = (preh[rng, :] - meanh[group]) * invh[group]
        preh[rng, :] = hat
        acth[rng, :] = silu(hat * gain + bias).astype(BF16)

    scores = mm(proj[...], acth[...], NT)
    row = lax.broadcasted_iota(jnp.int32, (16, LINE), 0)
    logits = jnp.where(row < NCLS, scores[0:16, :], -1e30)
    top = jnp.max(logits, axis=0, keepdims=True)
    power = jnp.where(row < NCLS, jnp.exp(logits - top), 0.0)
    soft = power / jnp.sum(power, axis=0, keepdims=True)
    onehot = (row == labels).astype(F32)
    d_logits = (soft - onehot) * (seg_keep / pixel_count(0))
    gap = scores[DEPTH_ROW:DEPTH_ROW + 1, :] - depth
    d_depth = depth_keep / pixel_count(1) * gap * lax.rsqrt(gap * gap + 1.0)
    guess = scores[NORMAL_ROW:NORMAL_ROW + 3, :]
    inverse = lax.rsqrt(jnp.sum(guess * guess, axis=0, keepdims=True) + 1.0)
    along = jnp.sum(guess * normals, axis=0, keepdims=True)
    weight = normal_keep / pixel_count(2)
    d_guess = r_("dscore")
    d_guess[...] = jnp.zeros(d_guess.shape, F32)
    d_guess[0:16, :] = d_logits
    d_guess[DEPTH_ROW:DEPTH_ROW + 1, :] = d_depth
    d_guess[NORMAL_ROW:NORMAL_ROW + 3, :] = -weight * (normals * inverse - along * (inverse * inverse * inverse) * guess)
    d_scores = d_guess[...]
    high = d_scores.astype(BF16)
    low = (d_scores - high.astype(F32)).astype(BF16)
    d_act = mm(high, proj[...], TN) + mm(low, proj[...], TN)
    value = mm(high, acth[...]) + mm(low, acth[...])
    d_proj = r_("dproj")
    d_proj[0:16, :] = value[0:16, 0:HEADW]
    d_proj[16:24, :] = value[16:24, HEADW:2 * HEADW]
    d_proj[24:32, :] = value[24:32, 2 * HEADW:]
    for group, rng in seg_rows(1):
        dyh[rng, :] = d_act[rng, :] * slope(preh[rng, :] * gain + bias)
    put_stats("th", 1, lambda g, rng: dyh[rng, :], lambda g, rng: dyh[rng, :] * preh[rng, :])
    sums = add_up("th")
    r_("head_vec_o")[...] = sums
    dph, dpx = r_("dph"), r_("dpx")
    for group, rng in seg_rows(1):
        first, second = sums[2 * group:2 * group + 1, :], sums[2 * group + 1:2 * group + 2, :]
        value = dyh[rng, :] - first / counts[group] - preh[rng, :] * (second / counts[group])
        dph[rng, :] = (gain * invh[group] * value).astype(BF16)

    slot = links.slots(12)
    place = rank % 4 + 1
    for step in range(TEAM):
        chip = team * TEAM + flip(rank, step)
        if step == 0:
            links.put_or_keep(dph, dpx.at[place, s], (seat, chip), slot + 2 * place + s, seat == s)
        else:
            links.put(dph, dpx.at[place, s], (seat, chip), slot + 2 * place + s)

    @pl.when(jnp.logical_not(has_low))
    def _():
        dpx[0] = jnp.zeros((2, LINE, HEADS), BF16)

    @pl.when(jnp.logical_not(has_high))
    def _():
        dpx[5] = jnp.zeros((2, LINE, HEADS), BF16)

    for index in range(2, 10):
        links.landed(dpx.at[index // 2, index % 2], slot + index)
    links.put(dpx.at[near_block], dpx.at[near_border], partner, slot + 2 * near_border)
    links.put(dpx.at[far_block], dpx.at[far_border], far_chip, slot + 2 * far_border, has_far)
    border_slot = slot

    dks, dkr, dku, dkg = r_("dks"), r_("dkr"), r_("dku"), r_("dkg")

    def tap_grad(tap, half):
        tap_row, tap_col = tap // 3, tap % 3
        acc = None
        for index in range(4):
            left = outs[tap_col, index + tap_row, half]
            right = dpx[index + 1].reshape(PIX, HEADS)
            if shape.borders:
                right = right * row_mask(first_block + index, tap_row).astype(BF16)
            term = mm(left, right, TN)
            acc = term if acc is None else acc + term
        return acc

    swap_slot, swap_out = links.slots(TAPS), links.outs(TAPS)

    def swap(tap):
        return links.copy(dks.at[tap], dkr.at[tap], partner, swap_out + tap, swap_slot + tap)

    def their_tap(tap, carry):
        dks[tap] = tap_grad(tap, other).astype(BF16)
        swap(tap).start()
        return carry

    lax.fori_loop(0, TAPS, their_tap, 0)
    links.open.append(lambda: lax.fori_loop(0, TAPS, lambda i, c: (swap(i).wait_send(), c)[1], 0))
    grad_slot = links.slots(teams * TAPS)
    grad_out = links.outs(TAPS * halves)

    def grad_copy(number):
        tap, place = number // halves, number % halves
        chunk = rank * share + s * halves + place
        overall = tap * dp + chunk
        owner, index = overall // TAPS, overall % TAPS
        src = dku.at[tap, pl.ds(pl.multiple_of(place * unit, unit), unit)]
        dst = dkg.at[team, index]
        at = grad_slot + team * TAPS + index
        to_core = jnp.where(owner == d, other, s)
        remote = lambda: links.copy(src, dst, (to_core, owner), grad_out + number, at)
        local = lambda: pltpu.make_async_copy(src, dst, links.recv.at[at])
        return owner == d, remote, local

    def grad_start(number):
        mine, remote, local = grad_copy(number)
        pl.when(mine)(lambda: local().start())
        pl.when(jnp.logical_not(mine))(lambda: remote().start())

    def grad_done(number):
        mine, remote, _ = grad_copy(number)
        pl.when(jnp.logical_not(mine))(lambda: remote().wait_send())

    def my_tap(tap, carry):
        value = tap_grad(tap, s)
        links.landed(dkr.at[tap], swap_slot + tap)
        dku[tap] = (value + dkr[tap].astype(F32)).astype(BF16)
        several(halves, lambda place: grad_start(tap * halves + place))
        return carry

    lax.fori_loop(0, TAPS, my_tap, 0)
    links.open.append(lambda: lax.fori_loop(0, TAPS * halves, lambda i, c: (grad_done(i), c)[1], 0))
    links.landed(dpx.at[0], border_slot, has_low)
    links.landed(dpx.at[5], border_slot + 10, has_high)

    dps, grads = r_("dps"), r_("grads")
    for task in range(3):
        cols = slice(task * HEADW, (task + 1) * HEADW)

        def spread(index, carry):
            piece = dpx[index, :, :, cols].reshape(PIX, HEADW)
            value = piece.astype(F32)
            dps[1, index] = piece
            dps[0, index] = sideways(value, 0).astype(BF16)
            dps[2, index] = sideways(value, 2).astype(BF16)
            return carry

        lax.fori_loop(0, 6, spread, 0)

        def pull(index, carry):
            acc = None
            for tap_row in range(3):
                for tap_col in range(3):
                    piece = dps[tap_col, index + tap_row]
                    if tap_row != 1 and shape.borders:
                        piece = piece * row_mask(first_block + index, tap_row).astype(BF16)
                    tap = 8 - (3 * tap_row + tap_col)
                    term = mm(piece, kernel[tap, :, :, cols].reshape(CH, HEADW), NT)
                    acc = term if acc is None else acc + term
            grads[task, index] = acc
            return carry

        lax.fori_loop(0, 4, pull, 0)

    pairs = [(i, j) for i in range(3) for j in range(i, 3)]

    def dots(index, sums):
        sums = list(sums)
        for group, rng in seg_rows(2):
            block = [grads[task, index, rng, :] for task in range(3)]
            for number, (i, j) in enumerate(pairs):
                sums[len(pairs) * group + number] += jnp.sum(block[i] * block[j], axis=0, keepdims=True)
        return tuple(sums)

    sums = lax.fori_loop(0, 4, dots, (jnp.zeros((1, CH), F32),) * (2 * len(pairs)))
    tally = jnp.zeros((8, LINE), F32)
    for number, total_row in enumerate(sums):
        tally = tally + jnp.where(lane == number, jnp.sum(total_row, axis=1, keepdims=True), 0.0)
    own_slot("gm")[...] = tally
    near_done = plane_sum("gm", None)


    far_done = line_sum("gm", near_done())
    gram_row = far_done()[0:1, :]
    dot_of = [jnp.sum(jnp.where(lane == k, gram_row, 0.0), axis=1, keepdims=True) for k in range(2 * len(pairs))]
    gram = {
        pair: jnp.where(lane == 0, dot_of[k], dot_of[len(pairs) + k]) for k, pair in enumerate(pairs)
    }
    alphas = jacobi_weights(gram)
    alphas = [[alpha[:, group:group + 1] for alpha in alphas] for group in range(2)]

    doutb, dout = r_("doutb"), r_("dout")
    slot = links.slots(4)
    for index in range(4):
        for group, rng in seg_rows(2):
            aligned = sum(alphas[group][task] * grads[task, index, rng, :] for task in range(3))
            doutb[index, rng, :] = aligned.astype(BF16)
        chip = team * TEAM + 4 * s + index
        links.put_or_keep(
            doutb.at[index], dout.at[rank % 4], (seat, chip), slot + rank % 4, (seat == s) & (rank % 4 == index)
        )

    own_slot("pj")[...] = d_proj[...]
    proj_near = plane_sum("pj", None)

    for index in range(4):
        links.landed(dout.at[index], slot + index)
    du, dpre3 = r_("du"), r_("dpre3")
    gain, bias = norm3
    for group, rng in seg_rows(2):
        at = slope(pre3[rng, :] * gain + bias + xh[rng, :].astype(F32))
        for part_index in range(4):
            cols = slice(part_index * CH, (part_index + 1) * CH)
            du[rng, cols] = dout[part_index, rng, :].astype(F32) * at[:, cols]
    vec = r_("vec_o")
    with_hat = lambda dy, hat: (lambda g, rng: dy[rng, :], lambda g, rng: dy[rng, :] * hat[rng, :])
    put_stats("t3", 2, *with_hat(du, pre3))
    sums = add_up("t3")
    vec[s, 0:1, :] = sums[1:2, :] + sums[3:4, :]
    vec[s, 1:2, :] = sums[0:1, :] + sums[2:3, :]

    def norm_back(sums, group, rng, dy, hat, scale):
        first, second = sums[2 * group:2 * group + 1, :], sums[2 * group + 1:2 * group + 2, :]
        return scale * (dy[rng, :] - first / counts[group] - hat[rng, :] * (second / counts[group]))

    for group, rng in seg_rows(2):
        dpre3[rng, :] = norm_back(sums, group, rng, du, pre3, gain * inv3[group]).astype(BF16)
    half2, half2r = r_("half2"), r_("half2r")
    value = mm(dpre3[...], take_rows(weights[2], 0, BOT), NT)
    half2[0], half2[1] = value[:, :HALF], value[:, HALF:]
    slot = links.slots()
    links.put(half2.at[other], half2r, partner, slot)

    def scatter(index):
        rows, wide = shape.rows[index], shape.wide[index]
        cut = rows // 2
        up, low = pl.ds(0, cut), pl.ds(cut, cut)
        buf = r_(f"dw{index}")
        ra, rb, rc = r_(f"ra{index}"), r_(f"rb{index}"), r_(f"rc{index}")
        slot = links.slots(6)
        links.put(buf.at[:, near_y, up], ra.at[0, :, 0], at_y, slot)
        links.put(buf.at[:, corner, up], ra.at[0, :, 1], at_y, slot + 1)
        links.put(buf.at[:, near_x, low], ra.at[1, :, 0], at_x, slot + 2)
        links.put(buf.at[:, corner, low], ra.at[1, :, 1], at_x, slot + 3)
        yield

        def add(at, part, extra):
            total = buf[:, at, part].astype(F32) + extra.astype(F32)
            buf[:, at, part] = total.astype(BF16)

        links.landed(ra.at[0, :, 1], slot + 1)
        add(near_x, up, ra[0, :, 1])
        links.put(buf.at[:, near_x, up], rb.at[0], at_x, slot + 4)
        links.landed(ra.at[1, :, 1], slot + 3)
        add(near_y, low, ra[1, :, 1])
        links.put(buf.at[:, near_y, low], rb.at[1], at_y, slot + 5)
        yield
        links.landed(ra.at[0, :, 0], slot)
        links.landed(ra.at[1, :, 0], slot + 2)
        links.landed(rb.at[0], slot + 4)
        add(spot, up, ra[0, :, 0].astype(F32) + rb[0].astype(F32))
        links.landed(rb.at[1], slot + 5)
        add(spot, low, ra[1, :, 0].astype(F32) + rb[1].astype(F32))
        first, out = links.slots(planes), links.outs(planes)

        def make(offset):
            to = (plane + offset) % planes
            return links.copy(buf.at[to, spot], rc.at[plane], (s, 4 * to + spot), out + offset, first + offset)

        several(planes - 1, lambda i: make(i + 1).start())
        links.open.append(lambda: several(planes - 1, lambda i: make(i + 1).wait_send()))
        rc[plane] = buf[plane, spot]
        yield
        several(planes - 1, lambda i: links.landed(rc.at[0], first + i + 1))
        acc = rc[0].astype(F32)
        for number in range(1, planes):
            acc = acc + rc[number].astype(F32)
        result = r_(f"dw{index}_o")
        mine = pl.ds(pl.multiple_of(s * wide, wide), wide)
        result[:, mine] = acc.astype(BF16)
        at = links.slots()
        links.put(result.at[:, mine], result.at[:, mine], partner, at)
        yield
        links.landed(result.at[:, mine], at)
        yield

    def advance(one):
        if one is not None:
            next(one)

    def reduced(index):
        if not shape.inside:
            return None
        one = scatter(index)
        next(one)
        return one

    grad_of = lambda index: r_(f"dw{index}") if shape.inside else r_(f"dw{index}_o")
    for half in range(2):
        put_rows(grad_of(2), half * HALF, mm(act2[half], dpre3[...], TN).astype(BF16))
    third = reduced(2)

    links.landed(half2r, slot)
    dy2, dp2 = r_("dy2"), r_("dp2")
    gain, bias = norm2
    for group, rng in seg_rows(2):
        value = half2[s, rng, :] + half2r[rng, :]
        dy2[rng, :] = value * slope(pre2[rng, :] * gain + bias)
    put_stats("t2", 2, *with_hat(dy2, pre2))
    sums = add_up("t2")
    vec[s, 2:3, 0:HALF] = sums[1:2, :] + sums[3:4, :]
    vec[s, 2:3, HALF:2 * HALF] = sums[0:1, :] + sums[2:3, :]
    for group, rng in seg_rows(2):
        dp2[1, rng, :] = norm_back(sums, group, rng, dy2, pre2, gain * inv2[group]).astype(BF16)
    slot = links.slots(2)
    links.put(dp2.at[1], dp2.at[2], (s, above), slot, has_above)
    links.put(dp2.at[1], dp2.at[0], (s, below), slot + 1, has_below)
    advance(third)

    @pl.when(jnp.logical_not(has_above))
    def _():
        dp2[0] = jnp.zeros((PIX, HALF), BF16)

    @pl.when(jnp.logical_not(has_below))
    def _():
        dp2[2] = jnp.zeros((PIX, HALF), BF16)

    for tap in range(TAPS):
        for half in range(2):
            at = tap * BOT + half * HALF
            put_rows(grad_of(1), at, mm(act1s[tap % 3, tap // 3, half], dp2[1], TN).astype(BF16))
    second = reduced(1)
    links.landed(dp2.at[2], slot, has_below)
    links.landed(dp2.at[0], slot + 1, has_above)
    acc = None
    for tap_row in range(3):
        value = dp2[tap_row].astype(F32)
        if tap_row != 1 and shape.borders:
            value = value * row_mask(d, tap_row)
        for tap_col in range(3):
            tap = 8 - (3 * tap_row + tap_col)
            term = mm(sideways(value, tap_col).astype(BF16), take_rows(weights[1], tap * BOT, BOT), NT)
            acc = term if acc is None else acc + term
    half1, half1r = r_("half1"), r_("half1r")
    half1[0], half1[1] = acc[:, :HALF], acc[:, HALF:]
    slot = links.slots()
    links.put(half1.at[other], half1r, partner, slot)
    advance(third)
    links.landed(half1r, slot)
    dy1, dp1 = r_("dy1"), r_("dp1")
    gain, bias = norm1
    for group, rng in seg_rows(2):
        value = half1[s, rng, :] + half1r[rng, :]
        dy1[rng, :] = value * slope(pre1[rng, :] * gain + bias)
    put_stats("t1", 2, *with_hat(dy1, pre1))
    sums = add_up("t1")
    vec[s, 2:3, 2 * HALF:3 * HALF] = sums[1:2, :] + sums[3:4, :]
    vec[s, 2:3, 3 * HALF:4 * HALF] = sums[0:1, :] + sums[2:3, :]
    vec[s, 3:8, :] = jnp.zeros((5, WIDE), F32)
    vec_slot = links.slots()
    links.put(vec.at[s], vec.at[s], partner, vec_slot)
    for group, rng in seg_rows(2):
        dp1[s, rng, :] = norm_back(sums, group, rng, dy1, pre1, gain * inv1[group]).astype(BF16)
    slot = links.slots()
    links.put(dp1.at[s], dp1.at[s], partner, slot)
    for part_index in range(4):
        cols = slice(part_index * BOT, (part_index + 1) * BOT)
        put_rows(grad_of(0), part_index * BOT, mm(x[:, cols], dp1[s], TN).astype(BF16))
    first = reduced(0)
    advance(second)

    result = r_("dk_o")
    done_slot, done_out = links.slots(TAPS), links.outs(TAPS)

    def finish_unit(index):
        mine, _, _, _ = unit_at(index)
        final = lambda: links.copy(result.at[index], result.at[index], partner, done_out + index, done_slot + index)

        @pl.when(mine)
        def _():
            several(teams, lambda t: links.landed(dkg.at[0, 0], grad_slot + t * TAPS + index))
            acc = dkg[0, index].astype(F32)
            for number in range(1, teams):
                acc = acc + dkg[number, index].astype(F32)
            result[index] = acc.astype(BF16)
            final().start()

        return mine, final

    proj_done = line_sum("pj", proj_near())

    links.landed(r_("wback"), back_slot)
    links.landed(dp1.at[other], slot)
    value = mm(dp1[s], rows_half(s)[...].reshape(WIDE, HALF), NT)
    value = value + mm(dp1[other], r_("wback")[...].reshape(WIDE, HALF), NT) + du[...]
    for line in range(2):
        r_("small_grad_o")[line * WS:(line + 1) * WS, :] = value[line * LINE:line * LINE + WS, :]
        r_("large_grad_o")[line * WL:(line + 1) * WL, :] = value[line * LINE + WS:(line + 1) * LINE, :]
    advance(third)
    advance(first)
    advance(second)
    advance(first)
    advance(third)
    lax.fori_loop(0, TAPS, lambda i, c: (finish_unit(i), c)[1], 0)
    advance(second)

    def finished(index):
        mine, _, _, _ = unit_at(index)
        final = links.copy(result.at[index], result.at[index], partner, done_out + index, done_slot + index)
        pl.when(mine)(lambda: final.wait_send())
        pl.when(jnp.logical_not(mine))(lambda: links.landed(result.at[index], done_slot + index))

    advance(first)
    advance(second)
    advance(first)
    lax.fori_loop(0, TAPS, lambda i, c: (finished(i), c)[1], 0)
    r_("proj_o")[...] = proj_done()
    links.landed(vec.at[other], vec_slot)
    for index, out_part in enumerate(out_parts):
        links.landed(out_part, out_slot + index)
    links.close()
    used["send"], used["recv"] = links.used_send, links.used_recv


def body(
    reduce_weight,
    dilated_weight,
    expand_weight,
    reduce_gain,
    reduce_bias,
    dilated_gain,
    dilated_bias,
    expand_gain,
    expand_bias,
    head_conv,
    head_gain,
    head_bias,
    seg_proj,
    depth_proj,
    normal_proj,
    small_feats,
    small_labels,
    small_depth,
    small_normals,
    small_depth_valid,
    small_normal_valid,
    large_feats,
    large_labels,
    large_depth,
    large_normals,
    large_depth_valid,
    large_normal_valid,
):
    dp = lax.axis_size("dp")
    section = lax.axis_index("section")
    assert small_feats.shape[0] == 2 * WS and large_feats.shape[0] == 2 * WL
    shape = Shapes(dp)

    if not shape.inside:
        def whole(shard, wide):
            mine = lax.dynamic_slice_in_dim(shard, section * wide, wide, 1)
            return lax.all_gather(mine, "dp", axis=0, tiled=True)

        reduce_weight = whole(reduce_weight, HALF)
        dilated_weight = whole(dilated_weight, HALF)
        expand_weight = whole(expand_weight, WIDE)

    vmem = pl.BlockSpec(memory_space=pltpu.VMEM)
    anywhere = pl.BlockSpec(memory_space=pl.ANY)
    flat = lambda value: value.reshape(1, -1)
    inputs = {
        "reduce_w": reduce_weight,
        "dilated_w": dilated_weight,
        "expand_w": expand_weight,
        "head_w": head_conv.reshape(TAPS, shape.unit, HEADS),
        "reduce_gain": flat(reduce_gain),
        "reduce_bias": flat(reduce_bias),
        "dilated_gain": flat(dilated_gain),
        "dilated_bias": flat(dilated_bias),
        "expand_gain": flat(expand_gain),
        "expand_bias": flat(expand_bias),
        "head_gain": head_gain.reshape(-1, 128),
        "head_bias": head_bias.reshape(-1, 128),
        "seg_proj": seg_proj.T,
        "depth_proj": depth_proj.T,
        "normal_proj": normal_proj.T,
        "small_feats": small_feats,
        "small_labels": flat(small_labels),
        "small_depth": flat(small_depth),
        "small_normals": small_normals,
        "small_depth_valid": flat(small_depth_valid),
        "small_normal_valid": flat(small_normal_valid),
        "large_feats": large_feats,
        "large_labels": flat(large_labels),
        "large_depth": flat(large_depth),
        "large_normals": large_normals,
        "large_depth_valid": flat(large_depth_valid),
        "large_normal_valid": flat(large_normal_valid),
    }
    outputs = {
        "small_out_o": ((2 * WS, C), BF16),
        "large_out_o": ((2 * WL, C), BF16),
        "small_grad_o": ((2 * WS, WIDE), F32),
        "large_grad_o": ((2 * WL, WIDE), F32),
        "dk_o": ((TAPS, shape.unit, HEADS), BF16),
        "vec_o": ((2, 8, WIDE), F32),
        "head_vec_o": ((4, HEADS), F32),
        "proj_o": ((PROJ, HEADW), F32),
    }
    for index in range(3):
        if shape.inside:
            outputs[f"dw{index}_o"] = ((shape.rows[index], 2 * shape.wide[index]), BF16)
        else:
            outputs[f"dw{index}_o"] = ((shape.full[index], shape.wide[index]), BF16)
    scratch = scratch_of(shape)
    scratch["dscore"] = ((PROJ, LINE), F32)
    names = [*inputs, *outputs, *scratch, "send", "recv"]
    used = {}

    def call(room, *operands):
        return pl.pallas_call(
            functools.partial(fused, shape, names, used),
            out_shape=[jax.ShapeDtypeStruct(dims, kind) for dims, kind in outputs.values()],
            in_specs=[anywhere if name == "head_w" else vmem for name in inputs],
            out_specs=[vmem] * len(outputs),
            scratch_shapes=[pltpu.VMEM(dims, kind) for dims, kind in scratch.values()]
            + [pltpu.SemaphoreType.DMA((count,)) for count in room],
            compiler_params=pltpu.CompilerParams(
                collective_id=0, has_side_effects=True, vmem_limit_bytes=64 * 2**20 - 2**16
            ),
            name="fused",
        )(*operands)

    jax.eval_shape(functools.partial(call, (2048, 2048)), *inputs.values())
    got = dict(zip(outputs, call((used["send"], used["recv"]), *inputs.values())))
    if not shape.inside:
        for index in range(3):
            mine = lax.psum_scatter(got[f"dw{index}_o"].astype(F32), "dp", scatter_dimension=0, tiled=True)
            both = lax.all_gather(mine, "section", axis=0)
            got[f"dw{index}_o"] = both.transpose(1, 0, 2).reshape(shape.rows[index], -1)

    results = {
        "small_out": ((2 * WS, C), BF16),
        "large_out": ((2 * WL, C), BF16),
        "small_grad": ((2 * WS, WIDE), F32),
        "large_grad": ((2 * WL, WIDE), F32),
        "dw0": ((shape.rows[0], BOT), F32),
        "dw1": ((shape.rows[1], BOT), F32),
        "dw2": ((shape.rows[2], C), F32),
        "reduce_gain": ((1, BOT), F32),
        "reduce_bias": ((1, BOT), F32),
        "dilated_gain": ((1, BOT), F32),
        "dilated_bias": ((1, BOT), F32),
        "expand_gain": ((1, C), F32),
        "expand_bias": ((1, C), F32),
        "dk": ((TAPS * shape.unit, HEADS), F32),
        "head_gain": ((HEADS // 128, 128), F32),
        "head_bias": ((HEADS // 128, 128), F32),
        "seg_proj": ((NCLS, HEADW), F32),
        "depth_proj": ((1, HEADW), F32),
        "normal_proj": ((3, HEADW), F32),
    }
    final = pl.pallas_call(
        functools.partial(finish, [*got, *results]),
        out_shape=[jax.ShapeDtypeStruct(dims, kind) for dims, kind in results.values()],
        in_specs=[vmem] * len(got),
        out_specs=[vmem] * len(results),
        compiler_params=pltpu.CompilerParams(vmem_limit_bytes=64 * 2**20 - 2**16),
        name="finish",
    )(*got.values())
    vectors = ("gain", "bias")
    return tuple(
        value.reshape(-1) if name.endswith(vectors) else value.T if name.endswith("proj") else value
        for name, value in zip(results, final)
    )


def finish(names, *refs):
    env = dict(zip(names, refs))
    for name in ("small_out", "large_out", "small_grad", "large_grad"):
        env[name][...] = env[name + "_o"][...]
    for index in range(3):
        env[f"dw{index}"][...] = env[f"dw{index}_o"][...].astype(F32)
    taps, unit, _ = env["dk_o"].shape
    for tap in range(taps):
        env["dk"][tap * unit:(tap + 1) * unit, :] = env["dk_o"][tap].astype(F32)
    vec, head_vec = env["vec_o"], env["head_vec_o"]
    for section in range(2):
        for row, name in enumerate(("expand_gain", "expand_bias")):
            env[name][0:1, section * WIDE:(section + 1) * WIDE] = vec[section, row:row + 1, :]
        for part, name in enumerate(("dilated_gain", "dilated_bias", "reduce_gain", "reduce_bias")):
            env[name][0:1, section * HALF:(section + 1) * HALF] = vec[section, 2:3, part * HALF:(part + 1) * HALF]
    gain = head_vec[1:2, :] + head_vec[3:4, :]
    bias = head_vec[0:1, :] + head_vec[2:3, :]
    for part in range(HEADS // 128):
        cols = slice(part * 128, (part + 1) * 128)
        env["head_gain"][part:part + 1, :] = gain[:, cols]
        env["head_bias"][part:part + 1, :] = bias[:, cols]
    proj = env["proj_o"]
    env["seg_proj"][...] = proj[0:NCLS, :]
    env["depth_proj"][...] = proj[DEPTH_ROW:DEPTH_ROW + 1, :]
    env["normal_proj"][...] = proj[NORMAL_ROW:NORMAL_ROW + 3, :]


def solution(mesh):
    rows, vector = P("dp", None), P()
    pixels, parts = P("dp"), P(None, "dp")
    group = (rows, pixels, pixels, parts, pixels, pixels)
    in_specs = (rows, rows, rows) + (vector,) * 6 + (rows,) + (vector,) * 5 + group + group
    out_specs = (
        (rows, rows, P("dp", "section"), P("dp", "section"), rows, rows, rows)
        + (vector,) * 6
        + (rows,)
        + (vector,) * 5
    )
    return jax.shard_map(body, mesh=mesh, in_specs=in_specs, out_specs=out_specs, check_vma=False)
```
